512 devices in a mesh: row: 16 (over z), col: 32 (over y, x, core).
Axes of the slice: x: 4, y: 4, z: 16, core: 2. Of those that a mesh axis runs over, the one named last changes fastest.
Arguments:
- points: float32 [16384, 128], P('row'), may hold values from -6 to 6
- panel_pool: float32 [16384, 128], P('col'), may hold values from -6 to 6
- order: int32 [512], replicated, may hold values from 0 to 511, each once
- panel_index: int32 [1], replicated, may hold values from 0 to 31
- inv_factor: float32 [512, 512], replicated, as said below
- ard_weights: float32 [128], replicated, may hold values from 0.001 to 0.1
- noise: float32 [16384], P('row'), may hold values from 0.05 to 1
Outputs:
- schur: float32 [16384, 16384], P('row', 'col')
The draws below stay inside these ranges and needn't reach their ends.
Inputs may be any that keep to these rules, and one draw needn't show every extreme that they name: `order`: a permutation of 0 to 511. `inv_factor`: lower triangular: zero above the diagonal.
All inputs are finite; a program needn't handle non-finite values.
Results may differ from the reference program's by a relative error of at most 0.0003.
Values sent between devices are 32-bit elements; how exact they have to be, the bound alone decides.
A program may use at most 64 MiB of HBM per device.

```python
import math
import jax
import jax.numpy as jnp
from jax import lax

FEATURES = 128
PANEL = 512
ROWS_DEV = 1024
TRAIL = 16384
PANELS = 32
POOL = 16384
N_ROW = 16


def draw_inv_factor(key, part):
    first_key, second_key = jax.random.split(jax.random.fold_in(key, 17))
    row_ids = lax.broadcasted_iota(jnp.int32, (PANEL, PANEL), 0)
    col_ids = lax.broadcasted_iota(jnp.int32, (PANEL, PANEL), 1)
    below = jax.random.normal(first_key, (PANEL, PANEL), jnp.float32) * (6.0 / PANEL)
    diagonal = jnp.exp(jax.random.uniform(second_key, (PANEL,), jnp.float32, math.log(0.1), math.log(0.4)))
    lower = jnp.where(row_ids > col_ids, below, jnp.float32(0.0))
    return lower + jnp.where(row_ids == col_ids, diagonal[:, None], jnp.float32(0.0))


def levels(stream_key, dims, shards, low, top_value):
    level, own = 1.0, jax.random.fold_in(stream_key, 6)
    for dim, parts in shards:
        draws = jnp.exp(jax.random.uniform(jax.random.fold_in(own, dim), (parts,), jnp.float32, low / len(shards), top_value / len(shards)))
        level = level * jnp.repeat(draws, dims[dim] // parts).reshape([-1 if axis == dim else 1 for axis in range(len(dims))])
    return level


def normal_values(own_key, extent, deviation, bound, pieces=(), kind=jnp.bfloat16):
    array = deviation * jax.random.normal(own_key, extent, jnp.float32)
    if pieces:
        array = array * levels(own_key, extent, pieces, -0.22, 0.18)
    return jnp.clip(array, -bound, bound).astype(kind)


def setup_inputs(seed: int = 0) -> dict:
    seeds = jax.random.split(jax.random.key(seed), 8)
    points = normal_values(seeds[0], (TRAIL, FEATURES), 1.0, 6.0, ((0, 16),), jnp.float32)
    panel_pool = normal_values(seeds[1], (POOL, FEATURES), 1.0, 6.0, ((0, 32),), jnp.float32)
    order = jax.random.permutation(seeds[2], PANEL).astype(jnp.int32)
    panel_index = jax.random.randint(seeds[3], (1,), 0, PANELS).astype(jnp.int32)
    inv_factor = draw_inv_factor(jax.random.fold_in(seeds[7], 71), 0)
    ard_weights = jnp.clip(jnp.exp(jax.random.uniform(seeds[5], (FEATURES,), jnp.float32, math.log(0.001), math.log(0.1))), 0.001, 0.1)
    noise = jnp.clip(jnp.exp(math.log(1.0) - 2.9957323 * jax.random.uniform(seeds[6], (TRAIL,), jnp.float32) ** levels(seeds[6], (TRAIL,), ((0, 16),), -0.2, 0.2)), 0.05, 1.0)
    return {"points": points, "panel_pool": panel_pool, "order": order, "panel_index": panel_index, "inv_factor": inv_factor, "ard_weights": ard_weights, "noise": noise}


amplitude = 2.0


def kernel_block(left_side, right_side, weights):
    scaled = left_side * weights[None, :]
    left_square = jnp.sum(scaled * left_side, axis=1)
    right_square = jnp.sum(right_side * right_side * weights[None, :], axis=1)
    cross_term = lax.dot_general(scaled, right_side, (((1,), (1,)), ((), ())), precision=lax.Precision.HIGHEST, preferred_element_type=jnp.float32)
    return amplitude * jnp.exp(-0.5 * (left_square[:, None] + right_square[None, :] - 2.0 * cross_term))


def factor_rows(row_points, chosen, inv_factor, weights):
    kernel_part = kernel_block(row_points, chosen, weights)
    return lax.dot_general(kernel_part, inv_factor, (((1,), (1,)), ((), ())), precision=lax.Precision.HIGHEST, preferred_element_type=jnp.float32)


def reference(points, panel_pool, order, panel_index, inv_factor, ard_weights, noise):
    start = (panel_index[0] * PANEL).astype(jnp.int32)
    block_points = lax.dynamic_slice_in_dim(panel_pool, start, PANEL, 0)
    chosen = jnp.take(block_points, order, axis=0)
    factored = factor_rows(points, chosen, inv_factor, ard_weights)

    def one_block(block_number):
        first = (block_number * ROWS_DEV).astype(jnp.int32)
        row_points = lax.dynamic_slice_in_dim(points, first, ROWS_DEV, 0)
        panel_part = lax.dynamic_slice_in_dim(factored, first, ROWS_DEV, 0)
        noise_part = lax.dynamic_slice_in_dim(noise, first, ROWS_DEV, 0)
        kernel_tile = kernel_block(row_points, points, ard_weights)
        row_ids = lax.broadcasted_iota(jnp.int32, (ROWS_DEV, TRAIL), 0) + first
        col_ids = lax.broadcasted_iota(jnp.int32, (ROWS_DEV, TRAIL), 1)
        kernel_tile = kernel_tile + jnp.where(row_ids == col_ids, noise_part[:, None], jnp.float32(0.0))
        update = lax.dot_general(panel_part, factored, (((1,), (1,)), ((), ())), precision=lax.Precision.HIGHEST, preferred_element_type=jnp.float32)
        return kernel_tile - update

    blocks = lax.map(one_block, jnp.arange(N_ROW, dtype=jnp.int32))
    return blocks.reshape(TRAIL, TRAIL)
```

```python
import functools

import jax
import jax.numpy as jnp
from jax import lax
from jax.experimental import pallas as pl
from jax.experimental.pallas import tpu as pltpu
from jax.sharding import PartitionSpec as P

MESH = pl.DeviceIdType.MESH
F32, BF16 = jnp.float32, jnp.bfloat16
FEAT = 128
PANEL = 512
ROWS = 1024
COLS = 512
NZ, NY, NX = 16, 4, 4
GROUP = NY * NX * 2
PIECE = PANEL // GROUP
SLICE = COLS // NY
REACH = 5


def dot_nt(a, b):
    return lax.dot_general(a, b, (((1,), (1,)), ((), ())), preferred_element_type=F32)


def dot_nn(a, b):
    return lax.dot_general(a, b, (((1,), (0,)), ((), ())), preferred_element_type=F32)


def split2(x):
    high = x.astype(BF16)
    return high, (x - high.astype(F32)).astype(BF16)


def split3(x):
    high = x.astype(BF16)
    rest = x - high.astype(F32)
    mid = rest.astype(BF16)
    return high, mid, (rest - mid.astype(F32)).astype(BF16)


def place():
    z, col = lax.axis_index("row"), lax.axis_index("col")
    return z, col // 8, col // 2 % 4, col % 2


def wrap(z):
    return lax.rem(z + NZ, NZ)


def gather_kernel(
    index_ref, order_ref, pool_ref, points_ref, col_out, chosen_out,
    mixed, landed, chosen, relay, cols,
    b_send, b_recv, one_send, one_recv, two_send, two_recv, local_sem,
):
    z, y, x, core = place()
    me = lax.axis_index("col")
    role = lax.rem(z - x + NZ, 4)
    home = 4 * y + x
    away = wrap(z - home)
    near = (away <= 2) | (away >= 14)
    holder = jnp.where(near, home, jnp.where(away <= 8, wrap(home + REACH), wrap(home - REACH)))
    group = jnp.where(role == 0, z, jnp.where(role == 1, wrap(z - REACH), wrap(z + REACH)))
    line = group // 4
    mine = line == y

    def column(y_place, core_place):
        return (y_place * 4 + x) * 2 + core_place

    barrier = pltpu.get_barrier_semaphore()

    @pl.when(role == 1)
    def _():
        pl.semaphore_signal(barrier, inc=1, device_id=(wrap(z - REACH), me), device_id_type=MESH)

    @pl.when(role == 3)
    def _():
        pl.semaphore_signal(barrier, inc=1, device_id=(wrap(z + REACH), me), device_id_type=MESH)

    for other in range(NY):
        @pl.when((away != 0) & ~((holder == z) & (other == y)))
        def _(other=other):
            pl.semaphore_signal(barrier, inc=1, device_id=(holder, column(other, core)), device_id_type=MESH)

    def greet(step, carry):
        pl.semaphore_signal(barrier, inc=1, device_id=(z, lax.rem(me + step, GROUP)), device_id_type=MESH)
        return carry

    lax.fori_loop(1, GROUP, greet, 0)

    pick = jnp.where(
        lax.broadcasted_iota(jnp.int32, (PANEL, PANEL), 0) == order_ref[...], 1.0, 0.0
    ).astype(BF16)
    parts = [
        lax.dot_general(pick, part, (((0,), (0,)), ((), ())), preferred_element_type=F32)
        for part in split3(pool_ref[...])
    ]
    mixed[...] = (parts[0] + parts[1]) + parts[2]

    expected = GROUP - 1 + jnp.where(
        role == 0, 6, jnp.where(role == 1, 6 - mine, jnp.where(role == 3, 5 - mine, 0))
    )
    pl.semaphore_wait(barrier, expected)

    own_slice = points_ref.at[pl.ds(pl.multiple_of(core * COLS + y * SLICE, SLICE), SLICE)]
    here = cols.at[pl.ds(pl.multiple_of(y * SLICE, SLICE), SLICE)]

    def leg_one(sign, place_id):
        return pltpu.make_async_remote_copy(
            src_ref=own_slice, dst_ref=relay, send_sem=one_send.at[place_id], recv_sem=one_recv,
            device_id=(wrap(z + sign * REACH), me), device_id_type=MESH,
        )

    def leg_two(source, offset, place_id):
        return pltpu.make_async_remote_copy(
            src_ref=source, dst_ref=here, send_sem=two_send.at[place_id], recv_sem=two_recv.at[y],
            device_id=(wrap(z + offset), column(line, core)), device_id_type=MESH,
        )

    @pl.when(role == 0)
    def _():
        leg_one(1, 0).start()
        leg_one(-1, 1).start()
        for place_id, offset in enumerate((-2, 2, -1, 1)):
            leg_two(own_slice, offset, place_id).start()

    def spread(step, carry):
        other = lax.rem(me + step, GROUP)
        pltpu.make_async_remote_copy(
            src_ref=mixed.at[pl.ds(pl.multiple_of(other * PIECE, PIECE), PIECE)],
            dst_ref=landed.at[me], send_sem=b_send.at[0], recv_sem=b_recv.at[0],
            device_id=(z, other), device_id_type=MESH,
        ).start()
        return carry

    lax.fori_loop(1, GROUP, spread, 0)
    my_rows = pl.ds(pl.multiple_of(me * PIECE, PIECE), PIECE)
    landed[me] = mixed[my_rows]
    whole = landed.at[pl.ds(0, GROUP - 1)]
    pltpu.make_async_copy(whole, whole, b_recv.at[0]).wait()
    chosen[my_rows] = landed[index_ref[0]]

    def share(step, carry):
        other = lax.rem(me + step, GROUP)
        pltpu.make_async_remote_copy(
            src_ref=chosen.at[my_rows], dst_ref=chosen.at[my_rows],
            send_sem=b_send.at[1], recv_sem=b_recv.at[1],
            device_id=(z, other), device_id_type=MESH,
        ).start()
        return carry

    lax.fori_loop(1, GROUP, share, 0)

    @pl.when((role == 1) | (role == 3))
    def _():
        leg_one(1, 0).wait_recv()
        for place_id, offset in enumerate((3, -2, 2, -1, 1, 0)):
            if offset == 3:
                wanted = role == 1
            elif offset == 0:
                wanted = ~mine
            else:
                wanted = None
            if wanted is None:
                leg_two(relay, offset, place_id).start()
            else:
                @pl.when(wanted)
                def _(offset=offset, place_id=place_id):
                    leg_two(relay, offset, place_id).start()

        @pl.when(mine)
        def _():
            pltpu.make_async_copy(relay, here, local_sem).start()
            pltpu.make_async_copy(relay, here, local_sem).wait()

    @pl.when(away == 0)
    def _():
        block = points_ref.at[pl.ds(pl.multiple_of(core * COLS, COLS), COLS)]
        pltpu.make_async_copy(block, cols, local_sem).start()
        pltpu.make_async_copy(block, cols, local_sem).wait()

    some = chosen.at[pl.ds(0, (GROUP - 1) * PIECE)]
    pltpu.make_async_copy(some, some, b_recv.at[1]).wait()
    chosen_out[...] = chosen[...]

    for other in range(NY):
        @pl.when((away != 0) & ~((holder == z) & (other == y)))
        def _(other=other):
            piece = cols.at[pl.ds(other * SLICE, SLICE)]
            pltpu.make_async_copy(piece, piece, two_recv.at[other]).wait()
    col_out[...] = cols[...]

    pltpu.make_async_copy(some, some, b_send.at[0]).wait()
    pltpu.make_async_copy(some, some, b_send.at[1]).wait()

    @pl.when(role == 0)
    def _():
        leg_one(1, 0).wait_send()
        leg_one(-1, 1).wait_send()
        for place_id, offset in enumerate((-2, 2, -1, 1)):
            leg_two(own_slice, offset, place_id).wait_send()

    @pl.when((role == 1) | (role == 3))
    def _():
        for place_id in range(1, 5):
            leg_two(relay, 1, place_id).wait_send()

        @pl.when(role == 1)
        def _():
            leg_two(relay, 3, 0).wait_send()

        @pl.when(~mine)
        def _():
            leg_two(relay, 0, 5).wait_send()


def gather_points(index, order, pool, points):
    shape = jax.ShapeDtypeStruct((PANEL, FEAT), F32)
    vmem = pl.BlockSpec(memory_space=pltpu.VMEM)
    return pl.pallas_call(
        gather_kernel,
        out_shape=(shape, shape),
        in_specs=[pl.BlockSpec(memory_space=pltpu.SMEM), vmem, vmem, pl.BlockSpec(memory_space=pl.ANY)],
        out_specs=(vmem, vmem),
        scratch_shapes=[
            pltpu.VMEM((PANEL, FEAT), F32),
            pltpu.VMEM((GROUP, PIECE, FEAT), F32),
            pltpu.VMEM((PANEL, FEAT), F32),
            pltpu.VMEM((SLICE, FEAT), F32),
            pltpu.VMEM((COLS, FEAT), F32),
            pltpu.SemaphoreType.DMA((2,)),
            pltpu.SemaphoreType.DMA((2,)),
            pltpu.SemaphoreType.DMA((2,)),
            pltpu.SemaphoreType.DMA,
            pltpu.SemaphoreType.DMA((6,)),
            pltpu.SemaphoreType.DMA((NY,)),
            pltpu.SemaphoreType.DMA,
        ],
        compiler_params=pltpu.CompilerParams(
            collective_id=0, has_side_effects=True, vmem_limit_bytes=24 * 2**20
        ),
        cost_estimate=pl.CostEstimate(flops=2 * 3 * PANEL * PANEL * FEAT, bytes_accessed=2**21, transcendentals=0),
        name="gather_points",
    )(index, order, pool, points)


def row_norms(scaled):
    return -0.5 * jnp.sum(scaled * scaled, axis=1, keepdims=True)


def column_norms(scaled):
    ones = jnp.ones((8, FEAT), F32)
    total = lax.dot_general(
        ones, scaled * scaled, (((1,), (1,)), ((), ())),
        precision=lax.Precision.HIGHEST, preferred_element_type=F32,
    )
    return -0.5 * total[0:1]


def sides(points, root):
    high, low = split2(points * root)
    kept = high.astype(F32) + low.astype(F32)
    return high, low, kept


def kern(left, right):
    left_high, left_low, left_norm = left
    right_high, right_low, right_norm = right
    pair = jnp.concatenate([left_high, left_low], axis=1)
    cross = dot_nt(pair, jnp.concatenate([right_high, right_high], axis=1))
    cross += dot_nt(pair, jnp.concatenate([right_low, right_low], axis=1))
    return 2.0 * jnp.exp(cross + left_norm + right_norm)


def triple_nt(a, b):
    return dot_nt(a[0], b[0]) + (dot_nt(a[0], b[1]) + dot_nt(a[1], b[0]))


def triple_nn(a, b):
    return dot_nn(a[0], b[0]) + (dot_nn(a[0], b[1]) + dot_nn(a[1], b[0]))


def tile_kernel(
    block, points_ref, col_ref, chosen_ref, inv_ref, weight_ref, noise_ref, out_ref,
    ch_high, ch_low, ch_norm, co_high, co_low, co_norm, h_high, h_low,
):
    z, col = lax.axis_index("row"), lax.axis_index("col")
    step = pl.program_id(0)
    root = jnp.sqrt(weight_ref[...])
    half = PANEL // 2

    @pl.when(step == 0)
    def _():
        high, low, kept = sides(chosen_ref[...], root)
        ch_high[...], ch_low[...], ch_norm[...] = high, low, column_norms(kept)
        high_c, low_c, kept_c = sides(col_ref[...], root)
        co_high[...], co_low[...], co_norm[...] = high_c, low_c, column_norms(kept_c)
        side = kern((high_c, low_c, row_norms(kept_c)), (high, low, ch_norm[...]))
        k_high, k_low = split2(side)
        inv = split2(inv_ref[...])
        first = triple_nt([k_high[:, :half], k_low[:, :half]], [w[:half, :half] for w in inv])
        second = triple_nt([k_high, k_low], [w[half:, :] for w in inv])
        first, second = split2(first), split2(second)
        both = [jnp.concatenate([a, b], axis=1) for a, b in zip(first, second)]
        left = triple_nn(both, [w[:, :half] for w in inv])
        right = triple_nn(second, [w[half:, half:] for w in inv])
        h_high[:, :half], h_low[:, :half] = split2(left)
        h_high[:, half:], h_low[:, half:] = split2(right)

    high, low, kept = sides(points_ref[...], root)
    norm = row_norms(kept)
    panel = split2(kern((high, low, norm), (ch_high[...], ch_low[...], ch_norm[...])))
    update = triple_nt(panel, (h_high[...], h_low[...]))
    tile = kern((high, low, norm), (co_high[...], co_low[...], co_norm[...]))
    row_ids = lax.broadcasted_iota(jnp.int32, (block, COLS), 0) + step * block + z * ROWS
    col_ids = lax.broadcasted_iota(jnp.int32, (block, COLS), 1) + col * COLS
    first_noise = pl.multiple_of(col % 2 * COLS, COLS)
    noise = noise_ref[:, pl.ds(first_noise, COLS)]
    out_ref[...] = tile + jnp.where(row_ids == col_ids, noise, 0.0) - update


def make_tile(points, cols, chosen, inv_factor, weights, noise):
    block = 256
    full = lambda shape: pl.BlockSpec(shape, lambda i: (0, 0))
    return pl.pallas_call(
        functools.partial(tile_kernel, block),
        grid=(ROWS // block,),
        out_shape=jax.ShapeDtypeStruct((ROWS, COLS), F32),
        in_specs=[
            pl.BlockSpec((block, FEAT), lambda i: (i, 0)),
            full((COLS, FEAT)), full((PANEL, FEAT)), full((PANEL, PANEL)), full((1, FEAT)), full((1, ROWS)),
        ],
        out_specs=pl.BlockSpec((block, COLS), lambda i: (i, 0)),
        scratch_shapes=[
            pltpu.VMEM((PANEL, FEAT), BF16), pltpu.VMEM((PANEL, FEAT), BF16), pltpu.VMEM((1, PANEL), F32),
            pltpu.VMEM((COLS, FEAT), BF16), pltpu.VMEM((COLS, FEAT), BF16), pltpu.VMEM((1, COLS), F32),
            pltpu.VMEM((COLS, PANEL), BF16), pltpu.VMEM((COLS, PANEL), BF16),
        ],
        compiler_params=pltpu.CompilerParams(vmem_limit_bytes=32 * 2**20),
        cost_estimate=pl.CostEstimate(flops=4 * 10**9, bytes_accessed=5 * 2**20, transcendentals=2**20),
        name="make_tile",
    )(points, cols, chosen, inv_factor, weights, noise)


def on_device(points, panel_pool, order, panel_index, inv_factor, ard_weights, noise):
    cols, chosen = gather_points(panel_index, order.reshape(1, PANEL), panel_pool, points)
    return make_tile(points, cols, chosen, inv_factor, ard_weights.reshape(1, FEAT), noise.reshape(1, ROWS))


def solution(mesh):
    in_specs = (P("row", None), P("col", None), P(), P(), P(), P(), P("row"))
    return jax.shard_map(
        on_device, mesh=mesh, in_specs=in_specs, out_specs=P("row", "col"), check_vma=False
    )
```

```python
import functools

import jax
import jax.numpy as jnp
from jax import lax
from jax.experimental import pallas as pl
from jax.experimental.pallas import tpu as pltpu
from jax.sharding import PartitionSpec as P

MESH = pl.DeviceIdType.MESH
F32, BF16 = jnp.float32, jnp.bfloat16
FEAT = 128
PANEL = 512
ROWS = 1024
COLS = 512
NZ, NY, NX = 16, 4, 4
SLICE = COLS // NY
TEAM = NY * 2
GROUP = NX * TEAM
PIECE = PANEL // GROUP
REACH = 5
SAME = 15
BLOCK = 256


def dot_nt(a, b):
    return lax.dot_general(a, b, (((1,), (1,)), ((), ())), preferred_element_type=F32)


def triple_nt(a, b):
    return dot_nt(a[0], b[0]) + (dot_nt(a[0], b[1]) + dot_nt(a[1], b[0]))


def dot_nn(a, b):
    return lax.dot_general(a, b, (((1,), (0,)), ((), ())), preferred_element_type=F32)


def triple_nn(a, b):
    return dot_nn(a[0], b[0]) + (dot_nn(a[0], b[1]) + dot_nn(a[1], b[0]))


def split2(x):
    high = x.astype(BF16)
    return high, (x - high.astype(F32)).astype(BF16)


def scaled_pair(points, root):
    high, low = split2(points * root)
    return jnp.concatenate([high, low], axis=1), high.astype(F32) + low.astype(F32)


def row_norms(kept):
    return -0.5 * jnp.sum(kept * kept, axis=1, keepdims=True)


def column_norms(kept):
    total = lax.dot_general(
        jnp.ones((8, FEAT), F32), kept * kept, (((1,), (1,)), ((), ())),
        precision=lax.Precision.HIGHEST, preferred_element_type=F32,
    )
    return -0.5 * total[0:1]


def kern(left, left_norm, right, right_norm):
    high, low = right[:, :FEAT], right[:, FEAT:]
    cross = dot_nt(left, jnp.concatenate([high, high], axis=1))
    cross += dot_nt(left, jnp.concatenate([low, low], axis=1))
    return 2.0 * jnp.exp(cross + left_norm + right_norm)


def column(y, x, core):
    return (y * NX + x) * 2 + core


def wrap(z):
    return lax.rem(z + NZ, NZ)


def gather_kernel(
    index_ref, order_ref, pool_ref, points_ref, inv_ref, weight_ref, noise_ref,
    col_out, pan_out, pan_norm, pair_out, norm_out, g_high, g_low, root_out, noise_out,
    order_v, points_v, inv_v, weight_v, w_high, w_low, landed, chosen, relay, cols,
    load_sem, ready_near, ready_plane, ready_plus, ready_minus, ready_two,
    one_send, one_recv, two_send, two_recv, b_send, b_recv,
):
    z, me = lax.axis_index("row"), lax.axis_index("col")
    y, x, core = me // 8, me // 2 % 4, me % 2
    seat = y * 2 + core
    home = NX * y + x
    role = wrap(z - x) % 4
    is_source = role == 0
    is_relay = (role == 1) | (role == 3)
    group = jnp.where(is_source, z, jnp.where(role == 1, wrap(z - REACH), wrap(z + REACH)))
    line = group // 4
    plus, minus = wrap(z + REACH), wrap(z - REACH)

    def skips(relay_place, target_place):
        return (relay_place >= NZ // 2) & (target_place < 4)

    away = wrap(z - home)
    middle = jnp.where(away <= 8, wrap(home + REACH), wrap(home - REACH))
    near = (away <= 2) | (away >= 14) | skips(middle, z)
    holder = jnp.where(near, home, middle)
    served = (away != 0) & (holder != z)

    def signal(sem, device):
        pl.semaphore_signal(sem, inc=1, device_id=device, device_id_type=MESH)

    def wait_for(sem, amount):
        @pl.when(amount > 0)
        def _():
            pl.semaphore_wait(sem, amount)

    def each(low, high, do):
        def body(i, carry):
            do(i)
            return carry
        lax.fori_loop(low, high, body, 0)

    def others(low, high, but, do):
        each(low, but, do)
        each(but + 1, high, do)

    def team(other):
        return (z, column(other // 2, x, other % 2))

    def across(other):
        return (z, column(y, other, core))

    def holders(other):
        return (holder, column(other, x, core))

    def target(place):
        return (place, column(line, x, core))

    own = [(is_source, wrap(z + o)) for o in (-2, 2, -1, 1)]
    skipped = []
    for d in range(3, 14):
        through = plus if d <= 8 else minus
        skipped.append((is_source & skips(through, wrap(z + d)), wrap(z + d)))
    passed = [
        ((role == 1 if o == 3 else is_relay) & ~skips(z, wrap(z + o)), wrap(z + o))
        for o in (3, -2, 2, -1, 1)
    ]
    first = own + skipped
    legs = [(is_source, plus), (is_source, minus)]
    sent = jnp.where(role == 1, minus, plus)

    def count(pairs, test):
        return sum(jnp.where(applies & test(place), 1, 0) for applies, place in pairs)

    lower = lambda place: place < z
    higher = lambda place: place > z

    barrier = pltpu.get_barrier_semaphore()

    @pl.when(served & (holder > z))
    def _():
        each(0, NY, lambda i: signal(barrier, holders(i)))

    @pl.when(is_relay & (sent > z))
    def _():
        signal(barrier, (sent, me))

    for applies, place in first + passed:
        @pl.when(applies & (place > z))
        def _(place=place):
            signal(barrier, target(place))

    for applies, place in legs:
        @pl.when(applies & (place > z))
        def _(place=place):
            signal(barrier, (place, me))

    each(seat + 1, TEAM, lambda i: signal(barrier, team(i)))
    each(x + 1, NX, lambda i: signal(barrier, across(i)))

    loads = [
        pltpu.make_async_copy(a, b, load_sem.at[i])
        for i, (a, b) in enumerate((
            (inv_ref, inv_v), (order_ref, order_v), (weight_ref, weight_v), (points_ref, points_v), (noise_ref, noise_out),
        ))
    ]
    for load in loads:
        load.start()

    expected = (
        seat + x + count(first + passed + legs, lower)
        + jnp.where(served & (holder < z), NY, 0) + jnp.where(is_relay & (sent < z), 1, 0)
    )
    wait_for(barrier, expected)

    own_slice = points_ref.at[pl.ds(pl.multiple_of(core * COLS + y * SLICE, SLICE), SLICE)]
    here = cols.at[pl.ds(pl.multiple_of(y * SLICE, SLICE), SLICE)]

    def leg_one(place, number):
        return pltpu.make_async_remote_copy(
            src_ref=own_slice, dst_ref=relay, send_sem=one_send.at[number], recv_sem=one_recv,
            device_id=(place, me), device_id_type=MESH,
        )

    def leg_two(from_ref, place, number):
        return pltpu.make_async_remote_copy(
            src_ref=from_ref, dst_ref=here, send_sem=two_send.at[number], recv_sem=two_recv.at[y],
            device_id=target(place), device_id_type=MESH,
        )

    def start_one(test):
        for number, (applies, place) in enumerate(legs):
            @pl.when(applies & test(number, place))
            def _(number=number, place=place):
                leg_one(place, number).start()

    def start_two(pairs, from_ref, test):
        for number, (applies, place) in enumerate(pairs):
            @pl.when(applies & test(place))
            def _(number=number, place=place):
                leg_two(from_ref, place, number).start()

    start_one(lambda number, place: place < z)
    start_two(first, own_slice, lower)

    each(0, seat, lambda i: signal(ready_near, team(i)))
    each(0, x, lambda i: signal(ready_near, across(i)))

    @pl.when(is_relay & (sent < z) & (role == 1))
    def _():
        signal(ready_plus, (sent, me))

    @pl.when(is_relay & (sent < z) & (role == 3))
    def _():
        signal(ready_minus, (sent, me))

    @pl.when(served & (holder < z))
    def _():
        each(0, NY, lambda i: signal(ready_two, holders(i)))

    wait_for(ready_near, (TEAM - 1 - seat) + (NX - 1 - x))
    others(0, NX, x, lambda i: signal(ready_plane, across(i)))
    pl.semaphore_wait(ready_plane, NX - 1)

    my_rows = pl.ds(pl.multiple_of(me * PIECE, PIECE), PIECE)

    def spread(step):
        other = lax.rem(me + step, GROUP)
        pltpu.make_async_remote_copy(
            src_ref=pool_ref.at[pl.ds(pl.multiple_of(other * PIECE, PIECE), PIECE)], dst_ref=landed.at[me],
            send_sem=b_send.at[0], recv_sem=b_recv.at[0], device_id=(z, other), device_id_type=MESH,
        ).start()

    def share(step):
        other = lax.rem(me + step, GROUP)
        pltpu.make_async_remote_copy(
            src_ref=chosen.at[my_rows], dst_ref=chosen.at[my_rows],
            send_sem=b_send.at[1], recv_sem=b_recv.at[1], device_id=(z, other), device_id_type=MESH,
        ).start()

    def wait_bytes(ref, sem):
        pltpu.make_async_copy(ref, ref, sem).wait()

    some = chosen.at[pl.ds(0, (GROUP - 1) * PIECE)]
    each(1, GROUP, spread)
    keep = pltpu.make_async_copy(pool_ref.at[my_rows], landed.at[me], load_sem.at[5])
    keep.start()

    loads[0].wait()
    loads[1].wait()
    pick = jnp.where(
        lax.broadcasted_iota(jnp.int32, (PANEL, PANEL), 0) == order_v[...], 1.0, 0.0
    ).astype(BF16)
    inv_high, inv_low = split2(inv_v[...])
    w_high[...] = dot_nt(inv_high, pick).astype(BF16)
    w_low[...] = dot_nt(inv_low, pick).astype(BF16)

    @pl.when(is_source & (plus > z))
    def _():
        pl.semaphore_wait(ready_plus, 1)
    start_one(lambda number, place: (place > z) & (number == 0))

    wait_bytes(some, b_recv.at[0])
    keep.wait()
    chosen[my_rows] = landed[index_ref[0]]
    each(1, GROUP, share)

    def pass_on():
        @pl.when(is_source & (minus > z))
        def _():
            pl.semaphore_wait(ready_minus, 1)
        start_one(lambda number, place: (place > z) & (number == 1))

        @pl.when(is_relay)
        def _():
            leg_one(plus, 0).wait_recv()
            start_two(passed, relay, lower)

            @pl.when(line != y)
            def _():
                leg_two(relay, z, SAME).start()

            @pl.when(line == y)
            def _():
                copy = pltpu.make_async_copy(relay, here, load_sem.at[0])
                copy.start()
                copy.wait()

        wait_for(ready_two, count(first + passed, higher))
        start_two(first, own_slice, higher)
        start_two(passed, relay, higher)

    @pl.when(z >= NZ // 2)
    def _():
        pass_on()

    loads[2].wait()
    loads[3].wait()
    root = jnp.sqrt(weight_v[...])
    root_out[...] = root
    pair, kept = scaled_pair(points_v[...], root)
    pair_out[...] = pair
    norm_out[...] = jnp.broadcast_to(row_norms(kept), (ROWS, FEAT))

    @pl.when(away == 0)
    def _():
        block = points_ref.at[pl.ds(pl.multiple_of(core * COLS, COLS), COLS)]
        copy = pltpu.make_async_copy(block, cols, load_sem.at[0])
        copy.start()
        copy.wait()

    wait_bytes(some, b_recv.at[1])

    @pl.when(z < NZ // 2)
    def _():
        pass_on()

    pan_pair, pan_kept = scaled_pair(chosen[...], root)
    pan_out[...] = pan_pair
    pan_norm[...] = column_norms(pan_kept)

    @pl.loop(0, ROWS // BLOCK)
    def _(step):
        rows = pl.ds(pl.multiple_of(step * BLOCK, BLOCK), BLOCK)
        part = split2(kern(pair_out[rows], norm_out[rows, 0:1], pan_out[...], pan_norm[...]))
        part = split2(triple_nt(part, (w_high[...], w_low[...])))
        g_high[rows], g_low[rows] = split2(triple_nn(part, (w_high[...], w_low[...])))

    for other in range(NY):
        @pl.when((away != 0) & ~((holder == z) & (other == y)))
        def _(other=other):
            wait_bytes(cols.at[pl.ds(other * SLICE, SLICE)], two_recv.at[other])

    col_out[...] = cols[...]

    wait_bytes(some, b_send.at[0])
    wait_bytes(some, b_send.at[1])
    for number, (applies, place) in enumerate(legs):
        @pl.when(applies)
        def _(number=number, place=place):
            leg_one(place, number).wait_send()
    for pairs, from_ref in ((first, own_slice), (passed, relay)):
        for number, (applies, place) in enumerate(pairs):
            @pl.when(applies)
            def _(number=number, place=place, from_ref=from_ref):
                leg_two(from_ref, place, number).wait_send()

    @pl.when(is_relay & (line != y))
    def _():
        leg_two(relay, z, SAME).wait_send()

    loads[4].wait()


def gather_points(index, order, pool, points, inv_factor, weights, noise):
    vmem = pl.BlockSpec(memory_space=pltpu.VMEM)
    hbm = pl.BlockSpec(memory_space=pltpu.HBM)
    shape = jax.ShapeDtypeStruct
    outs = (
        shape((COLS, FEAT), F32), shape((PANEL, 2 * FEAT), BF16), shape((1, PANEL), F32),
        shape((ROWS, 2 * FEAT), BF16), shape((ROWS, FEAT), F32),
        shape((ROWS, PANEL), BF16), shape((ROWS, PANEL), BF16), shape((1, FEAT), F32), shape((1, ROWS), F32),
    )
    dma, flag = pltpu.SemaphoreType.DMA, pltpu.SemaphoreType.REGULAR
    return pl.pallas_call(
        gather_kernel,
        out_shape=outs,
        in_specs=[pl.BlockSpec(memory_space=pltpu.SMEM)] + [hbm] * 6,
        out_specs=(vmem,) * len(outs),
        scratch_shapes=[
            pltpu.VMEM((1, PANEL), jnp.int32),
            pltpu.VMEM((ROWS, FEAT), F32),
            pltpu.VMEM((PANEL, PANEL), F32),
            pltpu.VMEM((1, FEAT), F32),
            pltpu.VMEM((PANEL, PANEL), BF16),
            pltpu.VMEM((PANEL, PANEL), BF16),
            pltpu.VMEM((GROUP, PIECE, FEAT), F32),
            pltpu.VMEM((PANEL, FEAT), F32),
            pltpu.VMEM((SLICE, FEAT), F32),
            pltpu.VMEM((COLS, FEAT), F32),
            dma((6,)),
            flag, flag, flag, flag, flag,
            dma((2,)),
            dma,
            dma((16,)),
            dma((NY,)),
            dma((2,)),
            dma((2,)),
        ],
        compiler_params=pltpu.CompilerParams(
            collective_id=0, has_side_effects=True, vmem_limit_bytes=40 * 2**20
        ),
        cost_estimate=pl.CostEstimate(flops=5 * 10**9, bytes_accessed=2**22, transcendentals=2**19),
        name="gather_points",
    )(index, order, pool, points, inv_factor, weights, noise)


def tile_kernel(
    col_ref, pan_ref, pan_norm, pair_ref, norm_ref, g_high, g_low, root_ref, noise_ref, out_ref, tile, out_sem,
):
    z, col = lax.axis_index("row"), lax.axis_index("col")
    pair, kept = scaled_pair(col_ref[...], root_ref[...])
    norms = column_norms(kept)
    side = split2(kern(pair, row_norms(kept), pan_ref[...], pan_norm[...]))
    noise = noise_ref[:, pl.ds(pl.multiple_of(col % 2 * COLS, COLS), COLS)]
    copies = []
    for step in range(ROWS // BLOCK):
        rows = pl.ds(step * BLOCK, BLOCK)
        update = triple_nt((g_high[rows], g_low[rows]), side)
        part = kern(pair_ref[rows], norm_ref[rows, 0:1], pair, norms)
        row_ids = lax.broadcasted_iota(jnp.int32, (BLOCK, COLS), 0) + (step * BLOCK + z * ROWS)
        col_ids = lax.broadcasted_iota(jnp.int32, (BLOCK, COLS), 1) + col * COLS
        tile[rows] = part + jnp.where(row_ids == col_ids, noise, 0.0) - update
        copy = pltpu.make_async_copy(tile.at[rows], out_ref.at[rows], out_sem.at[step])
        copy.start()
        copies.append(copy)
    for copy in copies:
        copy.wait()


def make_tile(parts):
    vmem = pl.BlockSpec(memory_space=pltpu.VMEM)
    return pl.pallas_call(
        tile_kernel,
        out_shape=jax.ShapeDtypeStruct((ROWS, COLS), F32),
        in_specs=[vmem] * len(parts),
        out_specs=pl.BlockSpec(memory_space=pltpu.HBM),
        scratch_shapes=[
            pltpu.VMEM((ROWS, COLS), F32),
            pltpu.SemaphoreType.DMA((ROWS // BLOCK,)),
        ],
        compiler_params=pltpu.CompilerParams(vmem_limit_bytes=40 * 2**20),
        cost_estimate=pl.CostEstimate(flops=3 * 10**9, bytes_accessed=2**22, transcendentals=2**19),
        name="make_tile",
    )(*parts)


def on_device(points, panel_pool, order, panel_index, inv_factor, ard_weights, noise):
    keep = lambda value: pltpu.with_memory_space_constraint(value, pltpu.HBM)
    return make_tile(gather_points(
        panel_index, keep(order.reshape(1, PANEL)), keep(panel_pool), keep(points), keep(inv_factor),
        keep(ard_weights.reshape(1, FEAT)), keep(noise.reshape(1, ROWS)),
    ))


def solution(mesh):
    in_specs = (P("row", None), P("col", None), P(), P(), P(), P(), P("row"))
    return jax.shard_map(
        on_device, mesh=mesh, in_specs=in_specs, out_specs=P("row", "col"), check_vma=False
    )
```

```python
import functools

import jax
import jax.numpy as jnp
from jax import lax
from jax.experimental import pallas as pl
from jax.experimental.pallas import tpu as pltpu
from jax.sharding import PartitionSpec as P

MESH = pl.DeviceIdType.MESH
F32, BF16 = jnp.float32, jnp.bfloat16
FEAT = 128
PANEL = 512
ROWS = 1024
COLS = 512
NZ, NY, NX = 16, 4, 4
SLICE = COLS // NY
GROUP = NX * NY * 2
PIECE = PANEL // GROUP
REACH = 5
SAME = 15
HALF = PANEL // 2
BLOCK = 512
TILE = 256


def dot_nt(a, b):
    return lax.dot_general(a, b, (((1,), (1,)), ((), ())), preferred_element_type=F32)


def triple_nt(a, b):
    return dot_nt(a[0], b[0]) + (dot_nt(a[0], b[1]) + dot_nt(a[1], b[0]))


def dot_nn(a, b):
    return lax.dot_general(a, b, (((1,), (0,)), ((), ())), preferred_element_type=F32)


def triple_nn(a, b):
    return dot_nn(a[0], b[0]) + (dot_nn(a[0], b[1]) + dot_nn(a[1], b[0]))


def split2(x):
    high = x.astype(BF16)
    return high, (x - high.astype(F32)).astype(BF16)


def split3(x):
    high = x.astype(BF16)
    rest = x - high.astype(F32)
    mid = rest.astype(BF16)
    return high, mid, (rest - mid.astype(F32)).astype(BF16)


def scaled_pair(points, root):
    high, low = split2(points * root)
    return jnp.concatenate([high, low], axis=1), high.astype(F32) + low.astype(F32)


def row_norms(kept):
    return -0.5 * jnp.sum(kept * kept, axis=1, keepdims=True)


def column_norms(kept):
    total = lax.dot_general(
        jnp.ones((8, FEAT), F32), kept * kept, (((1,), (1,)), ((), ())),
        precision=lax.Precision.HIGHEST, preferred_element_type=F32,
    )
    return -0.5 * total[0:1]


def kern(left, left_norm, right, right_norm):
    high, low = right[:, :FEAT], right[:, FEAT:]
    cross = dot_nt(left, jnp.concatenate([high, high], axis=1))
    cross += dot_nt(left, jnp.concatenate([low, low], axis=1))
    return 2.0 * jnp.exp(cross + left_norm + right_norm)


def column(y, x, core):
    return (y * NX + x) * 2 + core


def wrap(z):
    return lax.rem(z + NZ, NZ)


def gather_kernel(
    index_ref, order_ref, pool_ref, points_ref, inv_ref, weight_ref, noise_ref,
    col_out, pan_out, pan_norm, pair_out, norm_out, g_high, g_low, root_out, noise_out,
    order_v, points_v, inv_v, weight_v, pool_v, mixed, w_high, w_low, landed, chosen, relay, cols,
    load_sem, ready_plus, ready_minus, ready_two,
    one_send, one_recv, two_send, two_recv, b_send, b_recv,
):
    z, me = lax.axis_index("row"), lax.axis_index("col")
    y, x, core = me // 8, me // 2 % 4, me % 2
    home = NX * y + x
    role = wrap(z - x) % 4
    is_source = role == 0
    is_relay = (role == 1) | (role == 3)
    group = jnp.where(is_source, z, jnp.where(role == 1, wrap(z - REACH), wrap(z + REACH)))
    line = group // 4
    plus, minus = wrap(z + REACH), wrap(z - REACH)

    def skips(relay_place, target_place):
        return (relay_place >= NZ // 2) & (target_place < 4)

    away = wrap(z - home)
    middle = jnp.where(away <= 8, wrap(home + REACH), wrap(home - REACH))
    near = (away <= 2) | (away >= 14) | ((away > 8) & skips(middle, z))
    holder = jnp.where(near, home, middle)
    served = (away != 0) & (holder != z)

    def signal(sem, device):
        pl.semaphore_signal(sem, inc=1, device_id=device, device_id_type=MESH)

    def wait_for(sem, amount):
        @pl.when(amount > 0)
        def _():
            pl.semaphore_wait(sem, amount)

    def each(low, high, do):
        def body(i, carry):
            do(i)
            return carry
        lax.fori_loop(low, high, body, 0)

    def others(low, high, but, do):
        each(low, but, do)
        each(but + 1, high, do)

    def holders(other):
        return (holder, column(other, x, core))

    def target(place):
        return (place, column(line, x, core))

    own = [(is_source, wrap(z + o)) for o in (-2, 2, -1, 1)]
    skipped = []
    for d in range(9, 14):
        skipped.append((is_source & skips(minus, wrap(z + d)), wrap(z + d)))
    passed = [
        ((role == 1) | ((role == 3) & ~skips(z, wrap(z + o))) if o != 3 else role == 1, wrap(z + o))
        for o in (3, -2, 2, -1, 1)
    ]
    first = own + skipped
    legs = [(is_source, plus), (is_source, minus)]
    sent = jnp.where(role == 1, minus, plus)

    def count(pairs, test):
        return sum(jnp.where(applies & test(place), 1, 0) for applies, place in pairs)

    def tells(place):
        return (z < place) | (place >= NZ // 2)

    def knows(place):
        return (place < z) | (z >= NZ // 2)

    def unknown(place):
        return ~knows(place)

    barrier = pltpu.get_barrier_semaphore()

    @pl.when(served & tells(holder))
    def _():
        each(0, NY, lambda i: signal(barrier, holders(i)))

    @pl.when(is_relay & tells(sent))
    def _():
        signal(barrier, (sent, me))

    for applies, place in first + passed:
        @pl.when(applies & tells(place))
        def _(place=place):
            signal(barrier, target(place))

    for applies, place in legs:
        @pl.when(applies & tells(place))
        def _(place=place):
            signal(barrier, (place, me))

    each(1, GROUP, lambda i: signal(barrier, (z, lax.rem(me + i, GROUP))))

    loads = [
        pltpu.make_async_copy(a, b, load_sem.at[i])
        for i, (a, b) in enumerate((
            (inv_ref, inv_v), (order_ref, order_v), (weight_ref, weight_v), (points_ref, points_v), (noise_ref, noise_out),
            (pool_ref, pool_v),
        ))
    ]
    for load in loads:
        load.start()

    loads[1].wait()
    loads[5].wait()
    pick = jnp.where(
        lax.broadcasted_iota(jnp.int32, (PANEL, PANEL), 0) == order_v[...], 1.0, 0.0
    ).astype(BF16)
    parts = [
        lax.dot_general(pick, part, (((0,), (0,)), ((), ())), preferred_element_type=F32)
        for part in split3(pool_v[...])
    ]
    mixed[...] = (parts[0] + parts[1]) + parts[2]

    expected = (
        GROUP - 1 + count(first + passed + legs, knows)
        + jnp.where(served & knows(holder), NY, 0) + jnp.where(is_relay & knows(sent), 1, 0)
    )
    pl.semaphore_wait(barrier, expected)

    own_slice = points_ref.at[pl.ds(pl.multiple_of(core * COLS + y * SLICE, SLICE), SLICE)]
    here = cols.at[pl.ds(pl.multiple_of(y * SLICE, SLICE), SLICE)]

    def leg_one(place, number):
        return pltpu.make_async_remote_copy(
            src_ref=own_slice, dst_ref=relay, send_sem=one_send.at[number], recv_sem=one_recv,
            device_id=(place, me), device_id_type=MESH,
        )

    def leg_two(from_ref, place, number):
        return pltpu.make_async_remote_copy(
            src_ref=from_ref, dst_ref=here, send_sem=two_send.at[number], recv_sem=two_recv.at[y],
            device_id=target(place), device_id_type=MESH,
        )

    def start_one(test):
        for number, (applies, place) in enumerate(legs):
            @pl.when(applies & test(number, place))
            def _(number=number, place=place):
                leg_one(place, number).start()

    def start_two(pairs, from_ref, test):
        for number, (applies, place) in enumerate(pairs):
            @pl.when(applies & test(place))
            def _(number=number, place=place):
                leg_two(from_ref, place, number).start()

    start_one(lambda number, place: knows(place) & (place < NZ // 2))
    start_two(first, own_slice, lambda place: knows(place) & (wrap(place - z + 2) > 4))
    start_one(lambda number, place: knows(place) & (place >= NZ // 2))
    start_two(first, own_slice, lambda place: knows(place) & (wrap(place - z + 2) <= 4))

    @pl.when(is_relay & ~tells(sent) & (role == 1))
    def _():
        signal(ready_plus, (sent, me))

    @pl.when(is_relay & ~tells(sent) & (role == 3))
    def _():
        signal(ready_minus, (sent, me))

    @pl.when(served & ~tells(holder))
    def _():
        each(0, NY, lambda i: signal(ready_two, holders(i)))

    my_rows = pl.ds(pl.multiple_of(me * PIECE, PIECE), PIECE)

    def spread(step):
        other = lax.rem(me + step, GROUP)
        pltpu.make_async_remote_copy(
            src_ref=mixed.at[pl.ds(pl.multiple_of(other * PIECE, PIECE), PIECE)], dst_ref=landed.at[me],
            send_sem=b_send.at[0], recv_sem=b_recv.at[0], device_id=(z, other), device_id_type=MESH,
        ).start()

    def share(step):
        other = lax.rem(me + step, GROUP)
        pltpu.make_async_remote_copy(
            src_ref=chosen.at[my_rows], dst_ref=chosen.at[my_rows],
            send_sem=b_send.at[1], recv_sem=b_recv.at[1], device_id=(z, other), device_id_type=MESH,
        ).start()

    def wait_bytes(ref, sem):
        pltpu.make_async_copy(ref, ref, sem).wait()

    some = chosen.at[pl.ds(0, (GROUP - 1) * PIECE)]
    each(1, GROUP, spread)
    landed[me] = mixed[my_rows]

    loads[0].wait()
    w_high[...], w_low[...] = split2(inv_v[...])

    wait_bytes(some, b_recv.at[0])
    chosen[my_rows] = landed[index_ref[0]]
    each(1, GROUP, share)

    loads[2].wait()
    loads[3].wait()
    root = jnp.sqrt(weight_v[...])
    root_out[...] = root
    pair, kept = scaled_pair(points_v[...], root)
    pair_out[...] = pair
    norm_out[...] = jnp.broadcast_to(row_norms(kept), (ROWS, FEAT))

    @pl.when(away == 0)
    def _():
        block = points_ref.at[pl.ds(pl.multiple_of(core * COLS, COLS), COLS)]
        copy = pltpu.make_async_copy(block, cols, load_sem.at[0])
        copy.start()
        copy.wait()

    @pl.when(is_source)
    def _():
        for number, (place, ready) in enumerate(((plus, ready_plus), (minus, ready_minus))):
            @pl.when(unknown(place))
            def _(number=number, place=place, ready=ready):
                pl.semaphore_wait(ready, 1)
                leg_one(place, number).start()

        wait_for(ready_two, count(first, unknown))
        start_two(first, own_slice, unknown)

    @pl.when(is_relay)
    def _():
        leg_one(plus, 0).wait_recv()
        start_two(passed, relay, knows)

        @pl.when(line != y)
        def _():
            leg_two(relay, z, SAME).start()

        wait_for(ready_two, count(passed, unknown))
        start_two(passed, relay, unknown)

        @pl.when(line == y)
        def _():
            copy = pltpu.make_async_copy(relay, here, load_sem.at[0])
            copy.start()
            copy.wait()

    wait_bytes(some, b_recv.at[1])

    pan_pair, pan_kept = scaled_pair(chosen[...], root)
    pan_out[...] = pan_pair
    pan_norm[...] = column_norms(pan_kept)

    def factor(step, carry):
        rows = pl.ds(pl.multiple_of(step * BLOCK, BLOCK), BLOCK)
        part = split2(kern(pair_out[rows], norm_out[rows, 0:1], pan_out[...], pan_norm[...]))
        low, high = pl.ds(0, HALF), pl.ds(HALF, HALF)
        left = split2(triple_nt([k[:, :HALF] for k in part], (w_high[low, low], w_low[low, low])))
        right = split2(triple_nt(part, (w_high[high, :], w_low[high, :])))
        both = [jnp.concatenate(pair, axis=1) for pair in zip(left, right)]
        g_high[rows, low], g_low[rows, low] = split2(triple_nn(both, (w_high[:, low], w_low[:, low])))
        g_high[rows, high], g_low[rows, high] = split2(triple_nn(right, (w_high[high, high], w_low[high, high])))
        return carry

    lax.fori_loop(0, ROWS // BLOCK, factor, 0)

    for other in range(NY):
        @pl.when((away != 0) & ~((holder == z) & (other == y)))
        def _(other=other):
            wait_bytes(cols.at[pl.ds(other * SLICE, SLICE)], two_recv.at[other])

    col_out[...] = cols[...]

    wait_bytes(some, b_send.at[0])
    wait_bytes(some, b_send.at[1])
    for number, (applies, place) in enumerate(legs):
        @pl.when(applies)
        def _(number=number, place=place):
            leg_one(place, number).wait_send()
    for pairs, from_ref in ((first, own_slice), (passed, relay)):
        for number, (applies, place) in enumerate(pairs):
            @pl.when(applies)
            def _(number=number, place=place, from_ref=from_ref):
                leg_two(from_ref, place, number).wait_send()

    @pl.when(is_relay & (line != y))
    def _():
        leg_two(relay, z, SAME).wait_send()

    loads[4].wait()


def gather_points(index, order, pool, points, inv_factor, weights, noise):
    vmem = pl.BlockSpec(memory_space=pltpu.VMEM)
    hbm = pl.BlockSpec(memory_space=pltpu.HBM)
    shape = jax.ShapeDtypeStruct
    outs = (
        shape((COLS, FEAT), F32), shape((PANEL, 2 * FEAT), BF16), shape((1, PANEL), F32),
        shape((ROWS, 2 * FEAT), BF16), shape((ROWS, FEAT), F32),
        shape((ROWS, PANEL), BF16), shape((ROWS, PANEL), BF16), shape((1, FEAT), F32), shape((1, ROWS), F32),
    )
    dma, flag = pltpu.SemaphoreType.DMA, pltpu.SemaphoreType.REGULAR
    return pl.pallas_call(
        gather_kernel,
        out_shape=outs,
        in_specs=[pl.BlockSpec(memory_space=pltpu.SMEM)] + [hbm] * 6,
        out_specs=(vmem,) * len(outs),
        scratch_shapes=[
            pltpu.VMEM((1, PANEL), jnp.int32),
            pltpu.VMEM((ROWS, FEAT), F32),
            pltpu.VMEM((PANEL, PANEL), F32),
            pltpu.VMEM((1, FEAT), F32),
            pltpu.VMEM((PANEL, FEAT), F32),
            pltpu.VMEM((PANEL, FEAT), F32),
            pltpu.VMEM((PANEL, PANEL), BF16),
            pltpu.VMEM((PANEL, PANEL), BF16),
            pltpu.VMEM((GROUP, PIECE, FEAT), F32),
            pltpu.VMEM((PANEL, FEAT), F32),
            pltpu.VMEM((SLICE, FEAT), F32),
            pltpu.VMEM((COLS, FEAT), F32),
            dma((6,)),
            flag, flag, flag,
            dma((2,)),
            dma,
            dma((16,)),
            dma((NY,)),
            dma((2,)),
            dma((2,)),
        ],
        compiler_params=pltpu.CompilerParams(
            collective_id=0, has_side_effects=True, vmem_limit_bytes=40 * 2**20
        ),
        cost_estimate=pl.CostEstimate(flops=5 * 10**9, bytes_accessed=2**22, transcendentals=2**19),
        name="gather_points",
    )(index, order, pool, points, inv_factor, weights, noise)


def tile_kernel(
    col_ref, pan_ref, pan_norm, pair_ref, norm_ref, g_high, g_low, root_ref, noise_ref, out_ref, tile, out_sem,
):
    z, col = lax.axis_index("row"), lax.axis_index("col")
    pair, kept = scaled_pair(col_ref[...], root_ref[...])
    norms = column_norms(kept)
    side = split2(kern(pair, row_norms(kept), pan_ref[...], pan_norm[...]))
    noise = noise_ref[:, pl.ds(pl.multiple_of(col % 2 * COLS, COLS), COLS)]
    copies = []
    for step in range(ROWS // TILE):
        rows = pl.ds(step * TILE, TILE)
        update = triple_nt((g_high[rows], g_low[rows]), side)
        part = kern(pair_ref[rows], norm_ref[rows, 0:1], pair, norms)
        row_ids = lax.broadcasted_iota(jnp.int32, (TILE, COLS), 0) + (step * TILE + z * ROWS)
        col_ids = lax.broadcasted_iota(jnp.int32, (TILE, COLS), 1) + col * COLS
        tile[rows] = part + jnp.where(row_ids == col_ids, noise, 0.0) - update
        copy = pltpu.make_async_copy(tile.at[rows], out_ref.at[rows], out_sem.at[step])
        copy.start()
        copies.append(copy)
    for copy in copies:
        copy.wait()


def make_tile(parts):
    vmem = pl.BlockSpec(memory_space=pltpu.VMEM)
    return pl.pallas_call(
        tile_kernel,
        out_shape=jax.ShapeDtypeStruct((ROWS, COLS), F32),
        in_specs=[vmem] * len(parts),
        out_specs=pl.BlockSpec(memory_space=pltpu.HBM),
        scratch_shapes=[
            pltpu.VMEM((ROWS, COLS), F32),
            pltpu.SemaphoreType.DMA((ROWS // TILE,)),
        ],
        compiler_params=pltpu.CompilerParams(vmem_limit_bytes=40 * 2**20),
        cost_estimate=pl.CostEstimate(flops=3 * 10**9, bytes_accessed=2**22, transcendentals=2**19),
        name="make_tile",
    )(*parts)


def on_device(points, panel_pool, order, panel_index, inv_factor, ard_weights, noise):
    keep = lambda value: pltpu.with_memory_space_constraint(value, pltpu.HBM)
    return make_tile(gather_points(
        panel_index, keep(order.reshape(1, PANEL)), keep(panel_pool), keep(points), keep(inv_factor),
        keep(ard_weights.reshape(1, FEAT)), keep(noise.reshape(1, ROWS)),
    ))


def solution(mesh):
    in_specs = (P("row", None), P("col", None), P(), P(), P(), P(), P("row"))
    return jax.shard_map(
        on_device, mesh=mesh, in_specs=in_specs, out_specs=P("row", "col"), check_vma=False
    )
```

```python
import functools

import jax
import jax.numpy as jnp
from jax import lax
from jax.experimental import pallas as pl
from jax.experimental.pallas import tpu as pltpu
from jax.sharding import PartitionSpec as P

MESH = pl.DeviceIdType.MESH
F32, BF16 = jnp.float32, jnp.bfloat16
FEAT = 128
PANEL = 512
ROWS = 1024
COLS = 512
NZ, NY, NX = 16, 4, 4
SLICE = COLS // NY
GROUP = NX * NY * 2
PIECE = PANEL // GROUP
REACH = 5
SAME = 15
HALF = PANEL // 2
BLOCK = 512
TILE = 256


def dot_nt(a, b):
    return lax.dot_general(a, b, (((1,), (1,)), ((), ())), preferred_element_type=F32)


def triple_nt(a, b):
    return dot_nt(a[0], b[0]) + (dot_nt(a[0], b[1]) + dot_nt(a[1], b[0]))


def dot_nn(a, b):
    return lax.dot_general(a, b, (((1,), (0,)), ((), ())), preferred_element_type=F32)


def triple_nn(a, b):
    return dot_nn(a[0], b[0]) + (dot_nn(a[0], b[1]) + dot_nn(a[1], b[0]))


def split2(x):
    high = x.astype(BF16)
    return high, (x - high.astype(F32)).astype(BF16)


def split3(x):
    high = x.astype(BF16)
    rest = x - high.astype(F32)
    mid = rest.astype(BF16)
    return high, mid, (rest - mid.astype(F32)).astype(BF16)


def scaled_pair(points, root):
    high, low = split2(points * root)
    return jnp.concatenate([high, low], axis=1), high.astype(F32) + low.astype(F32)


def row_norms(kept):
    return -0.5 * jnp.sum(kept * kept, axis=1, keepdims=True)


def column_norms(kept):
    total = lax.dot_general(
        jnp.ones((8, FEAT), F32), kept * kept, (((1,), (1,)), ((), ())),
        precision=lax.Precision.HIGHEST, preferred_element_type=F32,
    )
    return -0.5 * total[0:1]


def kern(left, left_norm, right, right_norm):
    high, low = right[:, :FEAT], right[:, FEAT:]
    cross = dot_nt(left, jnp.concatenate([high, high], axis=1))
    cross += dot_nt(left, jnp.concatenate([low, low], axis=1))
    return 2.0 * jnp.exp(cross + left_norm + right_norm)


def column(y, x, core):
    return (y * NX + x) * 2 + core


def wrap(z):
    return lax.rem(z + NZ, NZ)


def gather_kernel(
    index_ref, order_ref, pool_ref, points_ref, inv_ref, weight_ref, noise_ref,
    col_out, pan_out, pan_norm, pair_out, norm_out, g_high, g_low, root_out, noise_out,
    order_v, points_v, inv_v, weight_v, pool_v, mixed, w_high, w_low, landed, chosen, relay, cols,
    load_sem, ready_plus, ready_minus, ready_two,
    one_send, one_recv, two_send, two_recv, b_send, b_recv,
):
    z, me = lax.axis_index("row"), lax.axis_index("col")
    y, x, core = me // 8, me // 2 % 4, me % 2
    home = NX * y + x
    role = wrap(z - x) % 4
    is_source = role == 0
    is_relay = (role == 1) | (role == 3)
    group = jnp.where(is_source, z, jnp.where(role == 1, wrap(z - REACH), wrap(z + REACH)))
    line = group // 4
    plus, minus = wrap(z + REACH), wrap(z - REACH)

    def skips(relay_place, target_place):
        return (relay_place >= NZ // 2) & (target_place < 4)

    away = wrap(z - home)
    middle = jnp.where(away <= 8, wrap(home + REACH), wrap(home - REACH))
    near = (away <= 2) | (away >= 14) | ((away > 8) & skips(middle, z))
    holder = jnp.where(near, home, middle)
    served = (away != 0) & (holder != z)

    def signal(sem, device):
        pl.semaphore_signal(sem, inc=1, device_id=device, device_id_type=MESH)

    def wait_for(sem, amount):
        @pl.when(amount > 0)
        def _():
            pl.semaphore_wait(sem, amount)

    def each(low, high, do):
        def body(i, carry):
            do(i)
            return carry
        lax.fori_loop(low, high, body, 0)

    def others(low, high, but, do):
        each(low, but, do)
        each(but + 1, high, do)

    def holders(other):
        return (holder, column(other, x, core))

    def target(place):
        return (place, column(line, x, core))

    own = [(is_source, wrap(z + o)) for o in (-2, 2, -1, 1)]
    skipped = []
    for d in range(9, 14):
        skipped.append((is_source & skips(minus, wrap(z + d)), wrap(z + d)))
    passed = [
        ((role == 1) | ((role == 3) & ~skips(z, wrap(z + o))) if o != 3 else role == 1, wrap(z + o))
        for o in (3, -2, 2, -1, 1)
    ]
    first = own + skipped
    legs = [(is_source, plus), (is_source, minus)]
    sent = jnp.where(role == 1, minus, plus)

    def count(pairs, test):
        return sum(jnp.where(applies & test(place), 1, 0) for applies, place in pairs)

    def tells(place):
        return (z < place) | (place >= NZ // 2)

    def knows(place):
        return (place < z) | (z >= NZ // 2)

    def unknown(place):
        return ~knows(place)

    barrier = pltpu.get_barrier_semaphore()
    each(1, GROUP, lambda i: signal(barrier, (z, lax.rem(me + i, GROUP))))

    loads = [
        pltpu.make_async_copy(a, b, load_sem.at[i])
        for i, (a, b) in enumerate((
            (inv_ref, inv_v), (order_ref, order_v), (weight_ref, weight_v), (points_ref, points_v), (noise_ref, noise_out),
            (pool_ref, pool_v),
        ))
    ]
    for load in loads:
        load.start()

    @pl.when(served & tells(holder))
    def _():
        each(0, NY, lambda i: signal(barrier, holders(i)))

    @pl.when(is_relay & tells(sent))
    def _():
        signal(barrier, (sent, me))

    for applies, place in first + passed:
        @pl.when(applies & tells(place))
        def _(place=place):
            signal(barrier, target(place))

    for applies, place in legs:
        @pl.when(applies & tells(place))
        def _(place=place):
            signal(barrier, (place, me))

    loads[1].wait()
    loads[5].wait()
    pick = jnp.where(
        lax.broadcasted_iota(jnp.int32, (PANEL, PANEL), 0) == order_v[...], 1.0, 0.0
    ).astype(BF16)
    parts = [
        lax.dot_general(pick, part, (((0,), (0,)), ((), ())), preferred_element_type=F32)
        for part in split3(pool_v[...])
    ]
    mixed[...] = (parts[0] + parts[1]) + parts[2]

    expected = (
        GROUP - 1 + count(first + passed + legs, knows)
        + jnp.where(served & knows(holder), NY, 0) + jnp.where(is_relay & knows(sent), 1, 0)
    )
    pl.semaphore_wait(barrier, expected)

    own_slice = points_ref.at[pl.ds(pl.multiple_of(core * COLS + y * SLICE, SLICE), SLICE)]
    here = cols.at[pl.ds(pl.multiple_of(y * SLICE, SLICE), SLICE)]

    def leg_one(place, number):
        return pltpu.make_async_remote_copy(
            src_ref=own_slice, dst_ref=relay, send_sem=one_send.at[number], recv_sem=one_recv,
            device_id=(place, me), device_id_type=MESH,
        )

    def leg_two(from_ref, place, number):
        return pltpu.make_async_remote_copy(
            src_ref=from_ref, dst_ref=here, send_sem=two_send.at[number], recv_sem=two_recv.at[y],
            device_id=target(place), device_id_type=MESH,
        )

    def start_one(test):
        for number, (applies, place) in enumerate(legs):
            @pl.when(applies & test(number, place))
            def _(number=number, place=place):
                leg_one(place, number).start()

    def start_two(pairs, from_ref, test):
        for number, (applies, place) in enumerate(pairs):
            @pl.when(applies & test(place))
            def _(number=number, place=place):
                leg_two(from_ref, place, number).start()

    def serve():
        start_one(lambda number, place: knows(place) & (place < NZ // 2))
        start_two(first, own_slice, lambda place: knows(place) & (wrap(place - z + 2) > 4))
        start_one(lambda number, place: knows(place) & (place >= NZ // 2))
        start_two(first, own_slice, lambda place: knows(place) & (wrap(place - z + 2) <= 4))

        @pl.when(is_relay & ~tells(sent) & (role == 1))
        def _():
            signal(ready_plus, (sent, me))

        @pl.when(is_relay & ~tells(sent) & (role == 3))
        def _():
            signal(ready_minus, (sent, me))

        @pl.when(served & ~tells(holder))
        def _():
            each(0, NY, lambda i: signal(ready_two, holders(i)))

    @pl.when(z >= NZ // 2)
    def _():
        serve()

    my_rows = pl.ds(pl.multiple_of(me * PIECE, PIECE), PIECE)

    def spread(step):
        other = lax.rem(me + step, GROUP)
        pltpu.make_async_remote_copy(
            src_ref=mixed.at[pl.ds(pl.multiple_of(other * PIECE, PIECE), PIECE)], dst_ref=landed.at[me],
            send_sem=b_send.at[0], recv_sem=b_recv.at[0], device_id=(z, other), device_id_type=MESH,
        ).start()

    def share(step):
        other = lax.rem(me + step, GROUP)
        pltpu.make_async_remote_copy(
            src_ref=chosen.at[my_rows], dst_ref=chosen.at[my_rows],
            send_sem=b_send.at[1], recv_sem=b_recv.at[1], device_id=(z, other), device_id_type=MESH,
        ).start()

    def wait_bytes(ref, sem):
        pltpu.make_async_copy(ref, ref, sem).wait()

    some = chosen.at[pl.ds(0, (GROUP - 1) * PIECE)]
    each(1, GROUP, spread)
    landed[me] = mixed[my_rows]

    @pl.when(z < NZ // 2)
    def _():
        serve()


    loads[0].wait()
    w_high[...], w_low[...] = split2(inv_v[...])

    wait_bytes(some, b_recv.at[0])
    chosen[my_rows] = landed[index_ref[0]]
    each(1, GROUP, share)

    loads[2].wait()
    loads[3].wait()
    root = jnp.sqrt(weight_v[...])
    root_out[...] = root
    pair, kept = scaled_pair(points_v[...], root)
    pair_out[...] = pair
    norm_out[...] = jnp.broadcast_to(row_norms(kept), (ROWS, FEAT))

    @pl.when(away == 0)
    def _():
        block = points_ref.at[pl.ds(pl.multiple_of(core * COLS, COLS), COLS)]
        copy = pltpu.make_async_copy(block, cols, load_sem.at[0])
        copy.start()
        copy.wait()

    @pl.when(is_source)
    def _():
        for number, (place, ready) in enumerate(((plus, ready_plus), (minus, ready_minus))):
            @pl.when(unknown(place))
            def _(number=number, place=place, ready=ready):
                pl.semaphore_wait(ready, 1)
                leg_one(place, number).start()

        wait_for(ready_two, count(first, unknown))
        start_two(first, own_slice, unknown)

    @pl.when(is_relay)
    def _():
        leg_one(plus, 0).wait_recv()
        start_two(passed, relay, knows)

        @pl.when(line != y)
        def _():
            leg_two(relay, z, SAME).start()

        wait_for(ready_two, count(passed, unknown))
        start_two(passed, relay, unknown)

        @pl.when(line == y)
        def _():
            copy = pltpu.make_async_copy(relay, here, load_sem.at[0])
            copy.start()
            copy.wait()

    wait_bytes(some, b_recv.at[1])

    pan_pair, pan_kept = scaled_pair(chosen[...], root)
    pan_out[...] = pan_pair
    pan_norm[...] = column_norms(pan_kept)

    def factor(step, carry):
        rows = pl.ds(pl.multiple_of(step * BLOCK, BLOCK), BLOCK)
        part = split2(kern(pair_out[rows], norm_out[rows, 0:1], pan_out[...], pan_norm[...]))
        low, high = pl.ds(0, HALF), pl.ds(HALF, HALF)
        left = split2(triple_nt([k[:, :HALF] for k in part], (w_high[low, low], w_low[low, low])))
        right = split2(triple_nt(part, (w_high[high, :], w_low[high, :])))
        both = [jnp.concatenate(pair, axis=1) for pair in zip(left, right)]
        g_high[rows, low], g_low[rows, low] = split2(triple_nn(both, (w_high[:, low], w_low[:, low])))
        g_high[rows, high], g_low[rows, high] = split2(triple_nn(right, (w_high[high, high], w_low[high, high])))
        return carry

    lax.fori_loop(0, ROWS // BLOCK, factor, 0)

    for other in range(NY):
        @pl.when((away != 0) & ~((holder == z) & (other == y)))
        def _(other=other):
            wait_bytes(cols.at[pl.ds(other * SLICE, SLICE)], two_recv.at[other])

    col_out[...] = cols[...]

    wait_bytes(some, b_send.at[0])
    wait_bytes(some, b_send.at[1])
    for number, (applies, place) in enumerate(legs):
        @pl.when(applies)
        def _(number=number, place=place):
            leg_one(place, number).wait_send()
    for pairs, from_ref in ((first, own_slice), (passed, relay)):
        for number, (applies, place) in enumerate(pairs):
            @pl.when(applies)
            def _(number=number, place=place, from_ref=from_ref):
                leg_two(from_ref, place, number).wait_send()

    @pl.when(is_relay & (line != y))
    def _():
        leg_two(relay, z, SAME).wait_send()

    loads[4].wait()


def gather_points(index, order, pool, points, inv_factor, weights, noise):
    vmem = pl.BlockSpec(memory_space=pltpu.VMEM)
    hbm = pl.BlockSpec(memory_space=pltpu.HBM)
    shape = jax.ShapeDtypeStruct
    outs = (
        shape((COLS, FEAT), F32), shape((PANEL, 2 * FEAT), BF16), shape((1, PANEL), F32),
        shape((ROWS, 2 * FEAT), BF16), shape((ROWS, FEAT), F32),
        shape((ROWS, PANEL), BF16), shape((ROWS, PANEL), BF16), shape((1, FEAT), F32), shape((1, ROWS), F32),
    )
    dma, flag = pltpu.SemaphoreType.DMA, pltpu.SemaphoreType.REGULAR
    return pl.pallas_call(
        gather_kernel,
        out_shape=outs,
        in_specs=[pl.BlockSpec(memory_space=pltpu.SMEM)] + [hbm] * 6,
        out_specs=(vmem,) * len(outs),
        scratch_shapes=[
            pltpu.VMEM((1, PANEL), jnp.int32),
            pltpu.VMEM((ROWS, FEAT), F32),
            pltpu.VMEM((PANEL, PANEL), F32),
            pltpu.VMEM((1, FEAT), F32),
            pltpu.VMEM((PANEL, FEAT), F32),
            pltpu.VMEM((PANEL, FEAT), F32),
            pltpu.VMEM((PANEL, PANEL), BF16),
            pltpu.VMEM((PANEL, PANEL), BF16),
            pltpu.VMEM((GROUP, PIECE, FEAT), F32),
            pltpu.VMEM((PANEL, FEAT), F32),
            pltpu.VMEM((SLICE, FEAT), F32),
            pltpu.VMEM((COLS, FEAT), F32),
            dma((6,)),
            flag, flag, flag,
            dma((2,)),
            dma,
            dma((16,)),
            dma((NY,)),
            dma((2,)),
            dma((2,)),
        ],
        compiler_params=pltpu.CompilerParams(
            collective_id=0, has_side_effects=True, vmem_limit_bytes=40 * 2**20
        ),
        cost_estimate=pl.CostEstimate(flops=5 * 10**9, bytes_accessed=2**22, transcendentals=2**19),
        name="gather_points",
    )(index, order, pool, points, inv_factor, weights, noise)


def tile_kernel(
    col_ref, pan_ref, pan_norm, pair_ref, norm_ref, g_high, g_low, root_ref, noise_ref, out_ref, tile, out_sem,
):
    z, col = lax.axis_index("row"), lax.axis_index("col")
    pair, kept = scaled_pair(col_ref[...], root_ref[...])
    norms = column_norms(kept)
    side = split2(kern(pair, row_norms(kept), pan_ref[...], pan_norm[...]))
    noise = noise_ref[:, pl.ds(pl.multiple_of(col % 2 * COLS, COLS), COLS)]
    copies = []
    for step in range(ROWS // TILE):
        rows = pl.ds(step * TILE, TILE)
        update = triple_nt((g_high[rows], g_low[rows]), side)
        part = kern(pair_ref[rows], norm_ref[rows, 0:1], pair, norms)
        row_ids = lax.broadcasted_iota(jnp.int32, (TILE, COLS), 0) + (step * TILE + z * ROWS)
        col_ids = lax.broadcasted_iota(jnp.int32, (TILE, COLS), 1) + col * COLS
        tile[rows] = part + jnp.where(row_ids == col_ids, noise, 0.0) - update
        copy = pltpu.make_async_copy(tile.at[rows], out_ref.at[rows], out_sem.at[step])
        copy.start()
        copies.append(copy)
    for copy in copies:
        copy.wait()


def make_tile(parts):
    vmem = pl.BlockSpec(memory_space=pltpu.VMEM)
    return pl.pallas_call(
        tile_kernel,
        out_shape=jax.ShapeDtypeStruct((ROWS, COLS), F32),
        in_specs=[vmem] * len(parts),
        out_specs=pl.BlockSpec(memory_space=pltpu.HBM),
        scratch_shapes=[
            pltpu.VMEM((ROWS, COLS), F32),
            pltpu.SemaphoreType.DMA((ROWS // TILE,)),
        ],
        compiler_params=pltpu.CompilerParams(vmem_limit_bytes=40 * 2**20),
        cost_estimate=pl.CostEstimate(flops=3 * 10**9, bytes_accessed=2**22, transcendentals=2**19),
        name="make_tile",
    )(*parts)


def on_device(points, panel_pool, order, panel_index, inv_factor, ard_weights, noise):
    keep = lambda value: pltpu.with_memory_space_constraint(value, pltpu.HBM)
    return make_tile(gather_points(
        panel_index, keep(order.reshape(1, PANEL)), keep(panel_pool), keep(points), keep(inv_factor),
        keep(ard_weights.reshape(1, FEAT)), keep(noise.reshape(1, ROWS)),
    ))


def solution(mesh):
    in_specs = (P("row", None), P("col", None), P(), P(), P(), P(), P("row"))
    return jax.shard_map(
        on_device, mesh=mesh, in_specs=in_specs, out_specs=P("row", "col"), check_vma=False
    )
```

```python
import functools

import jax
import jax.numpy as jnp
from jax import lax
from jax.experimental import pallas as pl
from jax.experimental.pallas import tpu as pltpu
from jax.sharding import PartitionSpec as P

MESH = pl.DeviceIdType.MESH
F32, BF16 = jnp.float32, jnp.bfloat16
FEAT = 128
PANEL = 512
ROWS = 1024
COLS = 512
NZ, NY, NX = 16, 4, 4
SLICE = COLS // NY
GROUP = NX * NY * 2
PIECE = PANEL // GROUP
REACH = 5
SAME = 15
HALF = PANEL // 2
BLOCK = 512
TILE = 256


def dot_nt(a, b):
    return lax.dot_general(a, b, (((1,), (1,)), ((), ())), preferred_element_type=F32)


def triple_nt(a, b):
    return dot_nt(jnp.concatenate([a[0], a[0], a[1]], axis=1), jnp.concatenate([b[0], b[1], b[0]], axis=1))


def dot_nn(a, b):
    return lax.dot_general(a, b, (((1,), (0,)), ((), ())), preferred_element_type=F32)


def triple_nn(a, b):
    return dot_nn(jnp.concatenate([a[0], a[0], a[1]], axis=1), jnp.concatenate([b[0], b[1], b[0]], axis=0))


def split2(x):
    high = x.astype(BF16)
    return high, (x - high.astype(F32)).astype(BF16)


def split3(x):
    high = x.astype(BF16)
    rest = x - high.astype(F32)
    mid = rest.astype(BF16)
    return high, mid, (rest - mid.astype(F32)).astype(BF16)


def scaled_pair(points, root):
    high, low = split2(points * root)
    return jnp.concatenate([high, low], axis=1), high.astype(F32) + low.astype(F32)


def row_norms(kept):
    return -0.5 * jnp.sum(kept * kept, axis=1, keepdims=True)


def column_norms(kept):
    total = lax.dot_general(
        jnp.ones((8, FEAT), F32), kept * kept, (((1,), (1,)), ((), ())),
        precision=lax.Precision.HIGHEST, preferred_element_type=F32,
    )
    return -0.5 * total[0:1]


def kern(left, left_norm, right, right_norm):
    high, low = right[:, :FEAT], right[:, FEAT:]
    cross = dot_nt(jnp.concatenate([left, left], axis=1), jnp.concatenate([high, high, low, low], axis=1))
    return 2.0 * jnp.exp(cross + left_norm + right_norm)


def column(y, x, core):
    return (y * NX + x) * 2 + core


def wrap(z):
    return lax.rem(z + NZ, NZ)


def gather_kernel(
    index_ref, order_ref, pool_ref, points_ref, inv_ref, weight_ref, noise_ref,
    col_out, pan_out, pan_norm, pair_out, norm_out, g_high, g_low, root_out, noise_out,
    order_v, points_v, inv_v, weight_v, pool_v, mixed, w_high, w_low, landed, chosen, relay, cols,
    load_sem, ready_plus, ready_minus, ready_two,
    one_send, one_recv, two_send, two_recv, b_send, b_recv,
):
    z, me = lax.axis_index("row"), lax.axis_index("col")
    y, x, core = me // 8, me // 2 % 4, me % 2
    home = NX * y + x
    role = wrap(z - x) % 4
    is_source = role == 0
    is_relay = (role == 1) | (role == 3)
    group = jnp.where(is_source, z, jnp.where(role == 1, wrap(z - REACH), wrap(z + REACH)))
    line = group // 4
    plus, minus = wrap(z + REACH), wrap(z - REACH)

    def skips(relay_place, target_place):
        return (relay_place >= NZ // 2) & (target_place < 4)

    away = wrap(z - home)
    middle = jnp.where(away <= 8, wrap(home + REACH), wrap(home - REACH))
    near = (away <= 2) | (away >= 14) | ((away > 8) & skips(middle, z))
    holder = jnp.where(near, home, middle)
    served = (away != 0) & (holder != z)

    def signal(sem, device):
        pl.semaphore_signal(sem, inc=1, device_id=device, device_id_type=MESH)

    def wait_for(sem, amount):
        @pl.when(amount > 0)
        def _():
            pl.semaphore_wait(sem, amount)

    def each(low, high, do):
        def body(i, carry):
            do(i)
            return carry
        lax.fori_loop(low, high, body, 0)

    def others(low, high, but, do):
        each(low, but, do)
        each(but + 1, high, do)

    def holders(other):
        return (holder, column(other, x, core))

    def target(place):
        return (place, column(line, x, core))

    own = [(is_source, wrap(z + o)) for o in (-2, 2, -1, 1)]
    skipped = []
    for d in range(9, 14):
        skipped.append((is_source & skips(minus, wrap(z + d)), wrap(z + d)))
    passed = [
        ((role == 1) | ((role == 3) & ~skips(z, wrap(z + o))) if o != 3 else role == 1, wrap(z + o))
        for o in (3, -2, 2, -1, 1)
    ]
    first = own + skipped
    legs = [(is_source, plus), (is_source, minus)]
    sent = jnp.where(role == 1, minus, plus)

    def count(pairs, test):
        return sum(jnp.where(applies & test(place), 1, 0) for applies, place in pairs)

    def tells(place):
        return (z < place) | (place >= NZ // 2)

    def knows(place):
        return (place < z) | (z >= NZ // 2)

    def unknown(place):
        return ~knows(place)

    barrier = pltpu.get_barrier_semaphore()

    @pl.when(served & tells(holder))
    def _():
        each(0, NY, lambda i: signal(barrier, holders(i)))

    @pl.when(is_relay & tells(sent))
    def _():
        signal(barrier, (sent, me))

    for applies, place in first + passed:
        @pl.when(applies & tells(place))
        def _(place=place):
            signal(barrier, target(place))

    for applies, place in legs:
        @pl.when(applies & tells(place))
        def _(place=place):
            signal(barrier, (place, me))

    each(1, GROUP, lambda i: signal(barrier, (z, lax.rem(me + i, GROUP))))

    loads = [
        pltpu.make_async_copy(a, b, load_sem.at[i])
        for i, (a, b) in enumerate((
            (inv_ref, inv_v), (order_ref, order_v), (weight_ref, weight_v), (points_ref, points_v), (noise_ref, noise_out),
            (pool_ref, pool_v),
        ))
    ]
    for load in loads:
        load.start()

    loads[1].wait()
    loads[5].wait()
    pick = jnp.where(
        lax.broadcasted_iota(jnp.int32, (PANEL, PANEL), 0) == order_v[...], 1.0, 0.0
    ).astype(BF16)
    parts = [
        lax.dot_general(pick, part, (((0,), (0,)), ((), ())), preferred_element_type=F32)
        for part in split3(pool_v[...])
    ]
    mixed[...] = (parts[0] + parts[1]) + parts[2]

    expected = (
        GROUP - 1 + count(first + passed + legs, knows)
        + jnp.where(served & knows(holder), NY, 0) + jnp.where(is_relay & knows(sent), 1, 0)
    )
    pl.semaphore_wait(barrier, expected)

    own_slice = points_ref.at[pl.ds(pl.multiple_of(core * COLS + y * SLICE, SLICE), SLICE)]
    here = cols.at[pl.ds(pl.multiple_of(y * SLICE, SLICE), SLICE)]

    def leg_one(place, number):
        return pltpu.make_async_remote_copy(
            src_ref=own_slice, dst_ref=relay, send_sem=one_send.at[number], recv_sem=one_recv,
            device_id=(place, me), device_id_type=MESH,
        )

    def leg_two(from_ref, place, number):
        return pltpu.make_async_remote_copy(
            src_ref=from_ref, dst_ref=here, send_sem=two_send.at[number], recv_sem=two_recv.at[y],
            device_id=target(place), device_id_type=MESH,
        )

    def start_one(test):
        for number, (applies, place) in enumerate(legs):
            @pl.when(applies & test(number, place))
            def _(number=number, place=place):
                leg_one(place, number).start()

    def start_two(pairs, from_ref, test):
        for number, (applies, place) in enumerate(pairs):
            @pl.when(applies & test(place))
            def _(number=number, place=place):
                leg_two(from_ref, place, number).start()

    start_one(lambda number, place: knows(place) & (place < NZ // 2))
    start_two(first, own_slice, lambda place: knows(place) & (wrap(place - z + 2) > 4))
    start_one(lambda number, place: knows(place) & (place >= NZ // 2))
    start_two(first, own_slice, lambda place: knows(place) & (wrap(place - z + 2) <= 4))

    @pl.when(is_relay & ~tells(sent) & (role == 1))
    def _():
        signal(ready_plus, (sent, me))

    @pl.when(is_relay & ~tells(sent) & (role == 3))
    def _():
        signal(ready_minus, (sent, me))

    @pl.when(served & ~tells(holder))
    def _():
        each(0, NY, lambda i: signal(ready_two, holders(i)))

    my_rows = pl.ds(pl.multiple_of(me * PIECE, PIECE), PIECE)

    def spread(step):
        other = lax.rem(me + step, GROUP)
        pltpu.make_async_remote_copy(
            src_ref=mixed.at[pl.ds(pl.multiple_of(other * PIECE, PIECE), PIECE)], dst_ref=landed.at[me],
            send_sem=b_send.at[0], recv_sem=b_recv.at[0], device_id=(z, other), device_id_type=MESH,
        ).start()

    def share(step):
        other = lax.rem(me + step, GROUP)
        pltpu.make_async_remote_copy(
            src_ref=chosen.at[my_rows], dst_ref=chosen.at[my_rows],
            send_sem=b_send.at[1], recv_sem=b_recv.at[1], device_id=(z, other), device_id_type=MESH,
        ).start()

    def wait_bytes(ref, sem):
        pltpu.make_async_copy(ref, ref, sem).wait()

    some = chosen.at[pl.ds(0, (GROUP - 1) * PIECE)]
    each(1, GROUP, spread)
    landed[me] = mixed[my_rows]

    loads[0].wait()
    w_high[...], w_low[...] = split2(inv_v[...])

    wait_bytes(some, b_recv.at[0])
    chosen[my_rows] = landed[index_ref[0]]
    each(1, GROUP, share)

    loads[2].wait()
    loads[3].wait()
    root = jnp.sqrt(weight_v[...])
    root_out[...] = root
    pair, kept = scaled_pair(points_v[...], root)
    pair_out[...] = pair
    norm_out[...] = jnp.broadcast_to(row_norms(kept), (ROWS, FEAT))

    @pl.when(away == 0)
    def _():
        block = points_ref.at[pl.ds(pl.multiple_of(core * COLS, COLS), COLS)]
        copy = pltpu.make_async_copy(block, cols, load_sem.at[0])
        copy.start()
        copy.wait()

    @pl.when(is_source)
    def _():
        for number, (place, ready) in enumerate(((plus, ready_plus), (minus, ready_minus))):
            @pl.when(unknown(place))
            def _(number=number, place=place, ready=ready):
                pl.semaphore_wait(ready, 1)
                leg_one(place, number).start()

        wait_for(ready_two, count(first, unknown))
        start_two(first, own_slice, unknown)

    @pl.when(is_relay)
    def _():
        leg_one(plus, 0).wait_recv()
        start_two(passed, relay, knows)

        @pl.when(line != y)
        def _():
            leg_two(relay, z, SAME).start()

        wait_for(ready_two, count(passed, unknown))
        start_two(passed, relay, unknown)

        @pl.when(line == y)
        def _():
            copy = pltpu.make_async_copy(relay, here, load_sem.at[0])
            copy.start()
            copy.wait()

    wait_bytes(some, b_recv.at[1])

    pan_pair, pan_kept = scaled_pair(chosen[...], root)
    pan_out[...] = pan_pair
    pan_norm[...] = column_norms(pan_kept)

    def factor(step, carry):
        rows = pl.ds(pl.multiple_of(step * BLOCK, BLOCK), BLOCK)
        part = split2(kern(pair_out[rows], norm_out[rows, 0:1], pan_out[...], pan_norm[...]))
        low, high = pl.ds(0, HALF), pl.ds(HALF, HALF)
        left = split2(triple_nt([k[:, :HALF] for k in part], (w_high[low, low], w_low[low, low])))
        right = split2(triple_nt(part, (w_high[high, :], w_low[high, :])))
        both = [jnp.concatenate(pair, axis=1) for pair in zip(left, right)]
        g_high[rows, low], g_low[rows, low] = split2(triple_nn(both, (w_high[:, low], w_low[:, low])))
        g_high[rows, high], g_low[rows, high] = split2(triple_nn(right, (w_high[high, high], w_low[high, high])))
        return carry

    lax.fori_loop(0, ROWS // BLOCK, factor, 0)

    for other in range(NY):
        @pl.when((away != 0) & ~((holder == z) & (other == y)))
        def _(other=other):
            wait_bytes(cols.at[pl.ds(other * SLICE, SLICE)], two_recv.at[other])

    col_out[...] = cols[...]

    wait_bytes(some, b_send.at[0])
    wait_bytes(some, b_send.at[1])
    for number, (applies, place) in enumerate(legs):
        @pl.when(applies)
        def _(number=number, place=place):
            leg_one(place, number).wait_send()
    for pairs, from_ref in ((first, own_slice), (passed, relay)):
        for number, (applies, place) in enumerate(pairs):
            @pl.when(applies)
            def _(number=number, place=place, from_ref=from_ref):
                leg_two(from_ref, place, number).wait_send()

    @pl.when(is_relay & (line != y))
    def _():
        leg_two(relay, z, SAME).wait_send()

    loads[4].wait()


def gather_points(index, order, pool, points, inv_factor, weights, noise):
    vmem = pl.BlockSpec(memory_space=pltpu.VMEM)
    hbm = pl.BlockSpec(memory_space=pltpu.HBM)
    shape = jax.ShapeDtypeStruct
    outs = (
        shape((COLS, FEAT), F32), shape((PANEL, 2 * FEAT), BF16), shape((1, PANEL), F32),
        shape((ROWS, 2 * FEAT), BF16), shape((ROWS, FEAT), F32),
        shape((ROWS, PANEL), BF16), shape((ROWS, PANEL), BF16), shape((1, FEAT), F32), shape((1, ROWS), F32),
    )
    dma, flag = pltpu.SemaphoreType.DMA, pltpu.SemaphoreType.REGULAR
    return pl.pallas_call(
        gather_kernel,
        out_shape=outs,
        in_specs=[pl.BlockSpec(memory_space=pltpu.SMEM)] + [hbm] * 6,
        out_specs=(vmem,) * len(outs),
        scratch_shapes=[
            pltpu.VMEM((1, PANEL), jnp.int32),
            pltpu.VMEM((ROWS, FEAT), F32),
            pltpu.VMEM((PANEL, PANEL), F32),
            pltpu.VMEM((1, FEAT), F32),
            pltpu.VMEM((PANEL, FEAT), F32),
            pltpu.VMEM((PANEL, FEAT), F32),
            pltpu.VMEM((PANEL, PANEL), BF16),
            pltpu.VMEM((PANEL, PANEL), BF16),
            pltpu.VMEM((GROUP, PIECE, FEAT), F32),
            pltpu.VMEM((PANEL, FEAT), F32),
            pltpu.VMEM((SLICE, FEAT), F32),
            pltpu.VMEM((COLS, FEAT), F32),
            dma((6,)),
            flag, flag, flag,
            dma((2,)),
            dma,
            dma((16,)),
            dma((NY,)),
            dma((2,)),
            dma((2,)),
        ],
        compiler_params=pltpu.CompilerParams(
            collective_id=0, has_side_effects=True, vmem_limit_bytes=40 * 2**20
        ),
        cost_estimate=pl.CostEstimate(flops=5 * 10**9, bytes_accessed=2**22, transcendentals=2**19),
        name="gather_points",
    )(index, order, pool, points, inv_factor, weights, noise)


def tile_kernel(
    col_ref, pan_ref, pan_norm, pair_ref, norm_ref, g_high, g_low, root_ref, noise_ref, out_ref, tile, out_sem,
):
    z, col = lax.axis_index("row"), lax.axis_index("col")
    pair, kept = scaled_pair(col_ref[...], root_ref[...])
    norms = column_norms(kept)
    side = split2(kern(pair, row_norms(kept), pan_ref[...], pan_norm[...]))
    noise = noise_ref[:, pl.ds(pl.multiple_of(col % 2 * COLS, COLS), COLS)]
    copies = []
    for step in range(ROWS // TILE):
        rows = pl.ds(step * TILE, TILE)
        update = triple_nt((g_high[rows], g_low[rows]), side)
        part = kern(pair_ref[rows], norm_ref[rows, 0:1], pair, norms)
        row_ids = lax.broadcasted_iota(jnp.int32, (TILE, COLS), 0) + (step * TILE + z * ROWS)
        col_ids = lax.broadcasted_iota(jnp.int32, (TILE, COLS), 1) + col * COLS
        tile[rows] = part + jnp.where(row_ids == col_ids, noise, 0.0) - update
        copy = pltpu.make_async_copy(tile.at[rows], out_ref.at[rows], out_sem.at[step])
        copy.start()
        copies.append(copy)
    for copy in copies:
        copy.wait()


def make_tile(parts):
    vmem = pl.BlockSpec(memory_space=pltpu.VMEM)
    return pl.pallas_call(
        tile_kernel,
        out_shape=jax.ShapeDtypeStruct((ROWS, COLS), F32),
        in_specs=[vmem] * len(parts),
        out_specs=pl.BlockSpec(memory_space=pltpu.HBM),
        scratch_shapes=[
            pltpu.VMEM((ROWS, COLS), F32),
            pltpu.SemaphoreType.DMA((ROWS // TILE,)),
        ],
        compiler_params=pltpu.CompilerParams(vmem_limit_bytes=40 * 2**20),
        cost_estimate=pl.CostEstimate(flops=3 * 10**9, bytes_accessed=2**22, transcendentals=2**19),
        name="make_tile",
    )(*parts)


def on_device(points, panel_pool, order, panel_index, inv_factor, ard_weights, noise):
    keep = lambda value: pltpu.with_memory_space_constraint(value, pltpu.HBM)
    return make_tile(gather_points(
        panel_index, keep(order.reshape(1, PANEL)), keep(panel_pool), keep(points), keep(inv_factor),
        keep(ard_weights.reshape(1, FEAT)), keep(noise.reshape(1, ROWS)),
    ))


def solution(mesh):
    in_specs = (P("row", None), P("col", None), P(), P(), P(), P(), P("row"))
    return jax.shard_map(
        on_device, mesh=mesh, in_specs=in_specs, out_specs=P("row", "col"), check_vma=False
    )
```

```python
import functools

import jax
import jax.numpy as jnp
from jax import lax
from jax.experimental import pallas as pl
from jax.experimental.pallas import tpu as pltpu
from jax.sharding import PartitionSpec as P

MESH = pl.DeviceIdType.MESH
F32, BF16 = jnp.float32, jnp.bfloat16
FEAT = 128
PANEL = 512
ROWS = 1024
COLS = 512
NZ, NY, NX = 16, 4, 4
SLICE = COLS // NY
GROUP = NX * NY * 2
PIECE = PANEL // GROUP
REACH = 5
SAME = 15
HALF = PANEL // 2
BLOCK = 512
TILE = 256


def dot_nt(a, b):
    return lax.dot_general(a, b, (((1,), (1,)), ((), ())), preferred_element_type=F32)


def triple_nt(a, b):
    return dot_nt(jnp.concatenate([a[0], a[0], a[1]], axis=1), jnp.concatenate([b[0], b[1], b[0]], axis=1))


def dot_nn(a, b):
    return lax.dot_general(a, b, (((1,), (0,)), ((), ())), preferred_element_type=F32)


def triple_nn(a, b):
    return dot_nn(jnp.concatenate([a[0], a[0], a[1]], axis=1), jnp.concatenate([b[0], b[1], b[0]], axis=0))


def split2(x):
    high = x.astype(BF16)
    return high, (x - high.astype(F32)).astype(BF16)


def split3(x):
    high = x.astype(BF16)
    rest = x - high.astype(F32)
    mid = rest.astype(BF16)
    return high, mid, (rest - mid.astype(F32)).astype(BF16)


def scaled_pair(points, root):
    high, low = split2(points * root)
    return jnp.concatenate([high, low], axis=1), high.astype(F32) + low.astype(F32)


def row_norms(kept):
    return -0.5 * jnp.sum(kept * kept, axis=1, keepdims=True)


def column_norms(kept):
    total = lax.dot_general(
        jnp.ones((8, FEAT), F32), kept * kept, (((1,), (1,)), ((), ())),
        precision=lax.Precision.HIGHEST, preferred_element_type=F32,
    )
    return -0.5 * total[0:1]


def kern(left, left_norm, right, right_norm):
    high, low = right[:, :FEAT], right[:, FEAT:]
    cross = dot_nt(jnp.concatenate([left, left], axis=1), jnp.concatenate([high, high, low, low], axis=1))
    return 2.0 * jnp.exp(cross + left_norm + right_norm)


def column(y, x, core):
    return (y * NX + x) * 2 + core


def wrap(z):
    return lax.rem(z + NZ, NZ)


def gather_kernel(
    index_ref, order_ref, pool_ref, points_ref, inv_ref, weight_ref, noise_ref,
    col_out, pan_out, pan_norm, pair_out, norm_out, g_high, g_low, root_out, noise_out,
    order_v, points_v, inv_v, weight_v, pool_v, mixed, w_high, w_low, landed, chosen, relay, cols,
    load_sem, ready_plus, ready_minus, ready_two,
    one_send, one_recv, two_send, two_recv, b_send, b_recv,
):
    z, me = lax.axis_index("row"), lax.axis_index("col")
    y, x, core = me // 8, me // 2 % 4, me % 2
    home = NX * y + x
    role = wrap(z - x) % 4
    is_source = role == 0
    is_relay = (role == 1) | (role == 3)
    group = jnp.where(is_source, z, jnp.where(role == 1, wrap(z - REACH), wrap(z + REACH)))
    line = group // 4
    plus, minus = wrap(z + REACH), wrap(z - REACH)

    def skips(relay_place, target_place):
        return (relay_place >= NZ // 2) & (target_place < 4)

    away = wrap(z - home)
    middle = jnp.where(away <= 8, wrap(home + REACH), wrap(home - REACH))
    near = (away <= 2) | (away >= 14) | ((away > 8) & skips(middle, z))
    holder = jnp.where(near, home, middle)
    served = (away != 0) & (holder != z)

    def signal(sem, device):
        pl.semaphore_signal(sem, inc=1, device_id=device, device_id_type=MESH)

    def wait_for(sem, amount):
        @pl.when(amount > 0)
        def _():
            pl.semaphore_wait(sem, amount)

    def each(low, high, do):
        def body(i, carry):
            do(i)
            return carry
        lax.fori_loop(low, high, body, 0)

    def others(low, high, but, do):
        each(low, but, do)
        each(but + 1, high, do)

    def holders(other):
        return (holder, column(other, x, core))

    def target(place):
        return (place, column(line, x, core))

    own = [(is_source, wrap(z + o)) for o in (-2, 2, -1, 1)]
    skipped = []
    for d in range(9, 14):
        skipped.append((is_source & skips(minus, wrap(z + d)), wrap(z + d)))
    passed = [
        ((role == 1) | ((role == 3) & ~skips(z, wrap(z + o))) if o != 3 else role == 1, wrap(z + o))
        for o in (3, -2, 2, -1, 1)
    ]
    first = own + skipped
    legs = [(is_source, plus), (is_source, minus)]
    sent = jnp.where(role == 1, minus, plus)

    def count(pairs, test):
        return sum(jnp.where(applies & test(place), 1, 0) for applies, place in pairs)

    def tells(place):
        return (z < place) | (place >= NZ // 2)

    def knows(place):
        return (place < z) | (z >= NZ // 2)

    def unknown(place):
        return ~knows(place)

    barrier = pltpu.get_barrier_semaphore()
    each(1, GROUP, lambda i: signal(barrier, (z, lax.rem(me + i, GROUP))))

    loads = [
        pltpu.make_async_copy(a, b, load_sem.at[i])
        for i, (a, b) in enumerate((
            (inv_ref, inv_v), (order_ref, order_v), (weight_ref, weight_v), (points_ref, points_v), (noise_ref, noise_out),
            (pool_ref, pool_v),
        ))
    ]
    for load in loads:
        load.start()

    @pl.when(served & tells(holder))
    def _():
        each(0, NY, lambda i: signal(barrier, holders(i)))

    @pl.when(is_relay & tells(sent))
    def _():
        signal(barrier, (sent, me))

    for applies, place in first + passed:
        @pl.when(applies & tells(place))
        def _(place=place):
            signal(barrier, target(place))

    for applies, place in legs:
        @pl.when(applies & tells(place))
        def _(place=place):
            signal(barrier, (place, me))

    loads[1].wait()
    loads[5].wait()
    pick = jnp.where(
        lax.broadcasted_iota(jnp.int32, (PANEL, PANEL), 0) == order_v[...], 1.0, 0.0
    ).astype(BF16)
    parts = [
        lax.dot_general(pick, part, (((0,), (0,)), ((), ())), preferred_element_type=F32)
        for part in split3(pool_v[...])
    ]
    mixed[...] = (parts[0] + parts[1]) + parts[2]

    expected = (
        GROUP - 1 + count(first + passed + legs, knows)
        + jnp.where(served & knows(holder), NY, 0) + jnp.where(is_relay & knows(sent), 1, 0)
    )
    pl.semaphore_wait(barrier, expected)

    own_slice = points_ref.at[pl.ds(pl.multiple_of(core * COLS + y * SLICE, SLICE), SLICE)]
    here = cols.at[pl.ds(pl.multiple_of(y * SLICE, SLICE), SLICE)]

    def leg_one(place, number):
        return pltpu.make_async_remote_copy(
            src_ref=own_slice, dst_ref=relay, send_sem=one_send.at[number], recv_sem=one_recv,
            device_id=(place, me), device_id_type=MESH,
        )

    def leg_two(from_ref, place, number):
        return pltpu.make_async_remote_copy(
            src_ref=from_ref, dst_ref=here, send_sem=two_send.at[number], recv_sem=two_recv.at[y],
            device_id=target(place), device_id_type=MESH,
        )

    def start_one(test):
        for number, (applies, place) in enumerate(legs):
            @pl.when(applies & test(number, place))
            def _(number=number, place=place):
                leg_one(place, number).start()

    def start_two(pairs, from_ref, test):
        for number, (applies, place) in enumerate(pairs):
            @pl.when(applies & test(place))
            def _(number=number, place=place):
                leg_two(from_ref, place, number).start()

    def serve():
        start_one(lambda number, place: knows(place) & (place < NZ // 2))
        start_two(first, own_slice, lambda place: knows(place) & (wrap(place - z + 2) > 4))
        start_one(lambda number, place: knows(place) & (place >= NZ // 2))
        start_two(first, own_slice, lambda place: knows(place) & (wrap(place - z + 2) <= 4))

        @pl.when(is_relay & ~tells(sent) & (role == 1))
        def _():
            signal(ready_plus, (sent, me))

        @pl.when(is_relay & ~tells(sent) & (role == 3))
        def _():
            signal(ready_minus, (sent, me))

        @pl.when(served & ~tells(holder))
        def _():
            each(0, NY, lambda i: signal(ready_two, holders(i)))

    @pl.when(z >= NZ // 2)
    def _():
        serve()

    my_rows = pl.ds(pl.multiple_of(me * PIECE, PIECE), PIECE)

    def spread(step):
        other = lax.rem(me + step, GROUP)
        pltpu.make_async_remote_copy(
            src_ref=mixed.at[pl.ds(pl.multiple_of(other * PIECE, PIECE), PIECE)], dst_ref=landed.at[me],
            send_sem=b_send.at[0], recv_sem=b_recv.at[0], device_id=(z, other), device_id_type=MESH,
        ).start()

    def share(step):
        other = lax.rem(me + step, GROUP)
        pltpu.make_async_remote_copy(
            src_ref=chosen.at[my_rows], dst_ref=chosen.at[my_rows],
            send_sem=b_send.at[1], recv_sem=b_recv.at[1], device_id=(z, other), device_id_type=MESH,
        ).start()

    def wait_bytes(ref, sem):
        pltpu.make_async_copy(ref, ref, sem).wait()

    some = chosen.at[pl.ds(0, (GROUP - 1) * PIECE)]
    each(1, GROUP, spread)
    landed[me] = mixed[my_rows]

    @pl.when(z < NZ // 2)
    def _():
        serve()


    loads[0].wait()
    w_high[...], w_low[...] = split2(inv_v[...])

    wait_bytes(some, b_recv.at[0])
    chosen[my_rows] = landed[index_ref[0]]
    each(1, GROUP, share)

    loads[2].wait()
    loads[3].wait()
    root = jnp.sqrt(weight_v[...])
    root_out[...] = root
    pair, kept = scaled_pair(points_v[...], root)
    pair_out[...] = pair
    norm_out[...] = jnp.broadcast_to(row_norms(kept), (ROWS, FEAT))

    @pl.when(away == 0)
    def _():
        block = points_ref.at[pl.ds(pl.multiple_of(core * COLS, COLS), COLS)]
        copy = pltpu.make_async_copy(block, cols, load_sem.at[0])
        copy.start()
        copy.wait()

    @pl.when(is_source)
    def _():
        for number, (place, ready) in enumerate(((plus, ready_plus), (minus, ready_minus))):
            @pl.when(unknown(place))
            def _(number=number, place=place, ready=ready):
                pl.semaphore_wait(ready, 1)
                leg_one(place, number).start()

        wait_for(ready_two, count(first, unknown))
        start_two(first, own_slice, unknown)

    @pl.when(is_relay)
    def _():
        leg_one(plus, 0).wait_recv()
        start_two(passed, relay, knows)

        @pl.when(line != y)
        def _():
            leg_two(relay, z, SAME).start()

        wait_for(ready_two, count(passed, unknown))
        start_two(passed, relay, unknown)

        @pl.when(line == y)
        def _():
            copy = pltpu.make_async_copy(relay, here, load_sem.at[0])
            copy.start()
            copy.wait()

    wait_bytes(some, b_recv.at[1])

    pan_pair, pan_kept = scaled_pair(chosen[...], root)
    pan_out[...] = pan_pair
    pan_norm[...] = column_norms(pan_kept)

    def factor(step, carry):
        rows = pl.ds(pl.multiple_of(step * BLOCK, BLOCK), BLOCK)
        part = split2(kern(pair_out[rows], norm_out[rows, 0:1], pan_out[...], pan_norm[...]))
        low, high = pl.ds(0, HALF), pl.ds(HALF, HALF)
        left = split2(triple_nt([k[:, :HALF] for k in part], (w_high[low, low], w_low[low, low])))
        right = split2(triple_nt(part, (w_high[high, :], w_low[high, :])))
        both = [jnp.concatenate(pair, axis=1) for pair in zip(left, right)]
        g_high[rows, low], g_low[rows, low] = split2(triple_nn(both, (w_high[:, low], w_low[:, low])))
        g_high[rows, high], g_low[rows, high] = split2(triple_nn(right, (w_high[high, high], w_low[high, high])))
        return carry

    lax.fori_loop(0, ROWS // BLOCK, factor, 0)

    for other in range(NY):
        @pl.when((away != 0) & ~((holder == z) & (other == y)))
        def _(other=other):
            wait_bytes(cols.at[pl.ds(other * SLICE, SLICE)], two_recv.at[other])

    col_out[...] = cols[...]

    wait_bytes(some, b_send.at[0])
    wait_bytes(some, b_send.at[1])
    for number, (applies, place) in enumerate(legs):
        @pl.when(applies)
        def _(number=number, place=place):
            leg_one(place, number).wait_send()
    for pairs, from_ref in ((first, own_slice), (passed, relay)):
        for number, (applies, place) in enumerate(pairs):
            @pl.when(applies)
            def _(number=number, place=place, from_ref=from_ref):
                leg_two(from_ref, place, number).wait_send()

    @pl.when(is_relay & (line != y))
    def _():
        leg_two(relay, z, SAME).wait_send()

    loads[4].wait()


def gather_points(index, order, pool, points, inv_factor, weights, noise):
    vmem = pl.BlockSpec(memory_space=pltpu.VMEM)
    hbm = pl.BlockSpec(memory_space=pltpu.HBM)
    shape = jax.ShapeDtypeStruct
    outs = (
        shape((COLS, FEAT), F32), shape((PANEL, 2 * FEAT), BF16), shape((1, PANEL), F32),
        shape((ROWS, 2 * FEAT), BF16), shape((ROWS, FEAT), F32),
        shape((ROWS, PANEL), BF16), shape((ROWS, PANEL), BF16), shape((1, FEAT), F32), shape((1, ROWS), F32),
    )
    dma, flag = pltpu.SemaphoreType.DMA, pltpu.SemaphoreType.REGULAR
    return pl.pallas_call(
        gather_kernel,
        out_shape=outs,
        in_specs=[pl.BlockSpec(memory_space=pltpu.SMEM)] + [hbm] * 6,
        out_specs=(vmem,) * len(outs),
        scratch_shapes=[
            pltpu.VMEM((1, PANEL), jnp.int32),
            pltpu.VMEM((ROWS, FEAT), F32),
            pltpu.VMEM((PANEL, PANEL), F32),
            pltpu.VMEM((1, FEAT), F32),
            pltpu.VMEM((PANEL, FEAT), F32),
            pltpu.VMEM((PANEL, FEAT), F32),
            pltpu.VMEM((PANEL, PANEL), BF16),
            pltpu.VMEM((PANEL, PANEL), BF16),
            pltpu.VMEM((GROUP, PIECE, FEAT), F32),
            pltpu.VMEM((PANEL, FEAT), F32),
            pltpu.VMEM((SLICE, FEAT), F32),
            pltpu.VMEM((COLS, FEAT), F32),
            dma((6,)),
            flag, flag, flag,
            dma((2,)),
            dma,
            dma((16,)),
            dma((NY,)),
            dma((2,)),
            dma((2,)),
        ],
        compiler_params=pltpu.CompilerParams(
            collective_id=0, has_side_effects=True, vmem_limit_bytes=40 * 2**20
        ),
        cost_estimate=pl.CostEstimate(flops=5 * 10**9, bytes_accessed=2**22, transcendentals=2**19),
        name="gather_points",
    )(index, order, pool, points, inv_factor, weights, noise)


def tile_kernel(
    col_ref, pan_ref, pan_norm, pair_ref, norm_ref, g_high, g_low, root_ref, noise_ref, out_ref, tile, out_sem,
):
    z, col = lax.axis_index("row"), lax.axis_index("col")
    pair, kept = scaled_pair(col_ref[...], root_ref[...])
    norms = column_norms(kept)
    side = split2(kern(pair, row_norms(kept), pan_ref[...], pan_norm[...]))
    noise = noise_ref[:, pl.ds(pl.multiple_of(col % 2 * COLS, COLS), COLS)]
    copies = []
    for step in range(ROWS // TILE):
        rows = pl.ds(step * TILE, TILE)
        update = triple_nt((g_high[rows], g_low[rows]), side)
        part = kern(pair_ref[rows], norm_ref[rows, 0:1], pair, norms)
        row_ids = lax.broadcasted_iota(jnp.int32, (TILE, COLS), 0) + (step * TILE + z * ROWS)
        col_ids = lax.broadcasted_iota(jnp.int32, (TILE, COLS), 1) + col * COLS
        tile[rows] = part + jnp.where(row_ids == col_ids, noise, 0.0) - update
        copy = pltpu.make_async_copy(tile.at[rows], out_ref.at[rows], out_sem.at[step])
        copy.start()
        copies.append(copy)
    for copy in copies:
        copy.wait()


def make_tile(parts):
    vmem = pl.BlockSpec(memory_space=pltpu.VMEM)
    return pl.pallas_call(
        tile_kernel,
        out_shape=jax.ShapeDtypeStruct((ROWS, COLS), F32),
        in_specs=[vmem] * len(parts),
        out_specs=pl.BlockSpec(memory_space=pltpu.HBM),
        scratch_shapes=[
            pltpu.VMEM((ROWS, COLS), F32),
            pltpu.SemaphoreType.DMA((ROWS // TILE,)),
        ],
        compiler_params=pltpu.CompilerParams(vmem_limit_bytes=40 * 2**20),
        cost_estimate=pl.CostEstimate(flops=3 * 10**9, bytes_accessed=2**22, transcendentals=2**19),
        name="make_tile",
    )(*parts)


def on_device(points, panel_pool, order, panel_index, inv_factor, ard_weights, noise):
    keep = lambda value: pltpu.with_memory_space_constraint(value, pltpu.HBM)
    return make_tile(gather_points(
        panel_index, keep(order.reshape(1, PANEL)), keep(panel_pool), keep(points), keep(inv_factor),
        keep(ard_weights.reshape(1, FEAT)), keep(noise.reshape(1, ROWS)),
    ))


def solution(mesh):
    in_specs = (P("row", None), P("col", None), P(), P(), P(), P(), P("row"))
    return jax.shard_map(
        on_device, mesh=mesh, in_specs=in_specs, out_specs=P("row", "col"), check_vma=False
    )
```
